32 devices in a mesh: grp: 2 (over y), stn: 4 (over z), chan: 4 (over x, core).
Axes of the slice: x: 2, y: 2, z: 4, core: 2. Of those that a mesh axis runs over, the one named last changes fastest.
Arguments:
- voltages: bfloat16 [256, 31, 8192], P(('grp', 'stn', 'chan')), parts along dimension 0, may hold values from -6 to 6
- taps: float32 [16, 8192], replicated, may hold values from -1.5 to 1.5
Outputs:
- visibilities: bfloat16 [8, 3, 256, 2, 1024], P(('grp', 'stn'), None, 'chan'), parts along dimension 0
The draws below stay inside these ranges and needn't reach their ends.
There are 2 independent parts, one for each index of `grp`. The reference program is written for one: setup_inputs(seed, part) draws one part's arguments, and reference() takes and returns one part's arrays. A program takes and returns all parts, laid end to end along the dimension named above; an argument that names none is the same for every part. Nothing has to cross between parts.
All inputs are finite; a program needn't handle non-finite values.
Results may differ from the reference program's by a relative error of at most 0.0053.
Values may be sent and summed in bfloat16 or wider, within the bound.
A program may use at most 64 MiB of HBM per device.

```python
import jax
import jax.numpy as jnp
from jax import lax

CHANNELS = 4096
TAPS = 16
AVG = 16
SPECTRA = 16
IN_DEV = 32
BLOCKS = 4
INPUTS = 128
FRAME_LEN = 8192
FRAMES = 31
REACH = 3
CH_OUT = 256
PAIRS = 1024


def block_levels(stream_key, extent, cuts, least, high):
    def one(dim, parts):
        draws = jax.random.uniform(jax.random.fold_in(jax.random.fold_in(stream_key, 6), dim), (parts,), jnp.float32, least / len(cuts), high / len(cuts))
        return jnp.repeat(jnp.exp(draws), extent[dim] // parts).reshape((-1,) + (1,) * (len(extent) - dim - 1))

    factor_of = one(*cuts[0])
    for cut in cuts[1:]:
        factor_of = factor_of * one(*cut)
    return factor_of


def normal_values(key, dims, spread, bound, split=(), held_as=jnp.bfloat16):
    factor_of = block_levels(key, dims, split, -0.22, 0.18) if split else 1.0
    entries = jax.random.normal(key, dims, jnp.float32) * spread * factor_of
    return jnp.minimum(jnp.maximum(entries, -bound), bound).astype(held_as)


def setup_inputs(seed: int = 0, part: int = 0) -> dict:
    seeds = jax.random.split(jax.random.key(seed), 3)
    part_keys = jax.random.split(jax.random.fold_in(seeds[2], part), 3)
    voltages = normal_values(part_keys[0], (INPUTS, FRAMES, FRAME_LEN), 1.0, 6.0, ((0, 16),))
    taps = normal_values(seeds[1], (TAPS, FRAME_LEN), TAPS ** -0.5, 1.5, (), jnp.float32)
    return dict(voltages=voltages, taps=taps)


def reference(voltages, taps):
    weighted = taps[0] * voltages[:, 0:SPECTRA, :].astype(jnp.float32)
    for tap_index in range(1, TAPS):
        weighted = weighted + taps[tap_index] * voltages[:, tap_index:tap_index + SPECTRA, :].astype(jnp.float32)
    spectrum = jnp.fft.rfft(weighted, axis=-1)[..., :CHANNELS] * (FRAME_LEN ** -0.5)
    real_part = lax.optimization_barrier(jnp.real(spectrum).astype(jnp.bfloat16)).astype(jnp.float32)
    imag_part = lax.optimization_barrier(jnp.imag(spectrum).astype(jnp.bfloat16)).astype(jnp.float32)
    stacked = jnp.concatenate([real_part, imag_part], axis=0)
    stacked = stacked.reshape(2, BLOCKS, IN_DEV, SPECTRA, CH_OUT, AVG)
    stacked = stacked.transpose(1, 4, 0, 2, 3, 5).reshape(BLOCKS, CH_OUT, 2 * IN_DEV, SPECTRA * AVG)
    scale = 1.0 / (SPECTRA * AVG)
    tiles = []
    for distance in range(REACH):
        other = jnp.roll(stacked, -distance, axis=0)
        product = jnp.einsum("ngak,ngck->ngac", stacked, other, precision=lax.Precision.HIGHEST)
        real_vis = product[:, :, :IN_DEV, :IN_DEV] + product[:, :, IN_DEV:, IN_DEV:]
        imag_vis = product[:, :, IN_DEV:, :IN_DEV] - product[:, :, :IN_DEV, IN_DEV:]
        both = jnp.stack([real_vis, imag_vis], axis=2).reshape(BLOCKS, CH_OUT, 2, PAIRS)
        tiles.append((both * scale).astype(jnp.bfloat16))
    return jnp.stack(tiles, axis=1)
```

```python
import functools
import math

import jax
import jax.numpy as jnp
import numpy as np
from jax import lax
from jax.experimental import pallas as pl
from jax.experimental.pallas import tpu as pltpu
from jax.sharding import PartitionSpec as P

AVG = 16


def from_behind(shard, axis, by):
    size = lax.axis_size(axis)
    return lax.ppermute(shard, axis, [(i, (i + by) % size) for i in range(size)])


def angle_table(rows, cols, modulus):
    product = (
        jnp.arange(rows, dtype=jnp.int32)[:, None]
        * jnp.arange(cols, dtype=jnp.int32)[None, :]
        % modulus
    )
    return 2.0 * math.pi / modulus * product.astype(jnp.float32)


def transform(weighted):
    rows_total = weighted.shape[0] * weighted.shape[1]
    frame_len = weighted.shape[2]
    inner = 128
    outer = frame_len // inner
    kept = frame_len // 2 // inner
    highest = lax.Precision.HIGHEST
    samples = weighted.reshape(rows_total, inner, outer)
    first = angle_table(inner, inner, inner)
    first_real = jnp.einsum("rqp,qk->rpk", samples, jnp.cos(first), precision=highest)
    first_imag = -jnp.einsum("rqp,qk->rpk", samples, jnp.sin(first), precision=highest)
    twist = angle_table(outer, inner, frame_len)
    twist_cos = jnp.cos(twist)
    twist_sin = jnp.sin(twist)
    second_real = first_real * twist_cos + first_imag * twist_sin
    second_imag = first_imag * twist_cos - first_real * twist_sin
    third = angle_table(outer, kept, outer)
    third_cos = jnp.cos(third)
    third_sin = jnp.sin(third)
    out_real = jnp.einsum("rpk,pm->rmk", second_real, third_cos, precision=highest) + jnp.einsum(
        "rpk,pm->rmk", second_imag, third_sin, precision=highest
    )
    out_imag = jnp.einsum("rpk,pm->rmk", second_imag, third_cos, precision=highest) - jnp.einsum(
        "rpk,pm->rmk", second_real, third_sin, precision=highest
    )
    scale = frame_len ** (-0.5)
    return (
        out_real.reshape(rows_total, kept * inner) * scale,
        out_imag.reshape(rows_total, kept * inner) * scale,
    )


def general(voltages, taps):
    inputs_here, frames, frame_len = voltages.shape
    tap_count = taps.shape[0]
    spectra_count = frames - tap_count + 1
    channels = frame_len // 2
    weighted = taps[0] * voltages[:, 0:spectra_count, :].astype(jnp.float32)
    for tap_index in range(1, tap_count):
        weighted = weighted + taps[tap_index] * voltages[
            :, tap_index : tap_index + spectra_count, :
        ].astype(jnp.float32)
    out_real, out_imag = transform(weighted)
    spectra = (
        jnp.stack([out_real, out_imag])
        .reshape(2, inputs_here, spectra_count, channels)
        .astype(jnp.bfloat16)
    )
    turned = lax.all_to_all(spectra, "chan", split_axis=3, concat_axis=1, tiled=True)
    block_inputs = turned.shape[1]
    chan_here = turned.shape[3]
    groups = chan_here // AVG
    scale = 1.0 / (spectra_count * AVG)
    half = lax.axis_size("stn") // 2
    reach = half + 1
    block = turned.reshape(2, block_inputs, spectra_count, groups, AVG)
    block = block.transpose(3, 0, 1, 2, 4).reshape(groups, 2 * block_inputs, spectra_count * AVG)

    def correlate(own, other):
        product = jnp.einsum("gak,gck->gac", own, other, preferred_element_type=jnp.float32)
        real_vis = (
            product[:, :block_inputs, :block_inputs] + product[:, block_inputs:, block_inputs:]
        )
        imag_vis = (
            product[:, block_inputs:, :block_inputs] - product[:, :block_inputs, block_inputs:]
        )
        both = jnp.stack([real_vis, imag_vis], axis=1).reshape(
            groups, 2, block_inputs * block_inputs
        )
        return (both * scale).astype(jnp.bfloat16)

    tiles = jnp.zeros((reach, groups, 2, block_inputs * block_inputs), jnp.bfloat16)
    tiles = tiles.at[0].set(correlate(block, block))

    def advance(distance, carry):
        moving, stack_now = carry
        moving = from_behind(moving, "stn", -1)
        stack_now = lax.dynamic_update_index_in_dim(
            stack_now, correlate(block, moving), distance, 0
        )
        return (moving, stack_now)

    moved, tiles = lax.fori_loop(1, reach, advance, (block, tiles))
    return tiles[None]


LANES = 128
SUB = 8
TILE = 16


def halves(table):
    high = table.astype(jnp.bfloat16)
    low = (table - high.astype(np.float64)).astype(jnp.bfloat16)
    return high, low


def fourier_tables(frame_len):
    outer = frame_len // LANES
    kept = frame_len // 2 // outer
    high_digit = np.arange(outer)
    lane = np.arange(LANES)
    first = 2.0 * np.pi / outer * (np.outer(high_digit, high_digit) % outer)
    first = np.concatenate([np.cos(first), -np.sin(first)], axis=0)
    high, low = halves(first)
    first = np.concatenate([high, low, high], axis=1)
    twist = 2.0 * np.pi / frame_len * (np.outer(high_digit, lane) % frame_len)
    last = 2.0 * np.pi / LANES * (np.outer(np.arange(kept), lane) % LANES)
    cos, sin = np.cos(last), np.sin(last)
    last = np.concatenate(
        [np.concatenate([cos, sin], axis=1), np.concatenate([-sin, cos], axis=1)], axis=0
    )
    high, low = halves(last * frame_len ** (-0.5))
    last = np.stack([high, low])
    return first, np.stack([np.cos(twist), np.sin(twist)]).astype(np.float32), last


def rows_by_rows(left, right):
    return lax.dot_general(
        left, right, (((1,), (1,)), ((), ())), preferred_element_type=jnp.float32
    )


def split(values):
    high = values.astype(jnp.bfloat16)
    return high, (values - high.astype(jnp.float32)).astype(jnp.bfloat16)


def spectra_kernel(v_ref, taps_ref, first_ref, twist_ref, last_ref, out_ref, frames, weighted, held):
    i = pl.program_id(0)
    tap_count = taps_ref.shape[0]
    frame_count = v_ref.shape[1]
    count = frame_count - tap_count + 1
    outer = v_ref.shape[2] // LANES
    kept = out_ref.shape[0]

    def filter_tile(tile, carry):
        lanes = pl.ds(pl.multiple_of(tile * LANES, LANES), LANES)
        frames[tile, 0:frame_count, :] = v_ref[0, :, lanes].astype(jnp.float32)
        total = taps_ref[0:1, lanes] * frames[tile, 0:count, :]
        for t in range(1, tap_count):
            total = total + taps_ref[t : t + 1, lanes] * frames[tile, t : t + count, :]
        weighted[pl.ds(tile, count, stride=outer), :] = total
        return carry

    lax.fori_loop(0, outer, filter_tile, 0, unroll=4)

    per_pass = 2 * LANES // outer
    for chunk in range(count // per_pass):
        parts = []
        for pair in range(per_pass // 2):
            s = chunk * per_pass + 2 * pair
            samples = jnp.concatenate(
                [weighted[s * outer : (s + 1) * outer, :], weighted[(s + 1) * outer : (s + 2) * outer, :]],
                axis=1,
            )
            high, low = split(samples)
            y = jnp.dot(
                first_ref[...],
                jnp.concatenate([high, high, low], axis=0),
                preferred_element_type=jnp.float32,
            )
            for k in range(2):
                real = y[:outer, k * LANES : (k + 1) * LANES]
                imag = y[outer:, k * LANES : (k + 1) * LANES]
                parts.append(
                    jnp.concatenate(
                        [
                            real * twist_ref[0] + imag * twist_ref[1],
                            imag * twist_ref[0] - real * twist_ref[1],
                        ],
                        axis=1,
                    )
                )
        high, low = split(jnp.concatenate(parts, axis=0))
        result = (
            rows_by_rows(last_ref[0], high)
            + rows_by_rows(last_ref[1], high)
            + rows_by_rows(last_ref[0], low)
        )
        for part in range(2):
            for k in range(2):
                held[chunk * 2 + k, pl.ds(part * SUB + i, kept, stride=TILE), :] = result[
                    part * kept : (part + 1) * kept, k * LANES : (k + 1) * LANES
                ]

    @pl.when(i == pl.num_programs(0) - 1)
    def _():
        for tile in range(held.shape[0]):
            out_ref[:, :, tile * LANES : (tile + 1) * LANES] = (
                held[tile].reshape(kept, TILE, LANES).astype(jnp.bfloat16)
            )


def local_spectra(voltages, taps):
    inputs_here, frame_count, frame_len = voltages.shape
    count = frame_count - taps.shape[0] + 1
    outer = frame_len // LANES
    kept = frame_len // 2 // outer
    tables = fourier_tables(frame_len)
    fixed = [taps] + [jnp.asarray(t) for t in tables]
    return pl.pallas_call(
        spectra_kernel,
        grid=(inputs_here,),
        in_specs=[pl.BlockSpec((1, frame_count, frame_len), lambda i: (i, 0, 0))]
        + [pl.BlockSpec(a.shape, lambda i, n=a.ndim: (0,) * n) for a in fixed],
        out_specs=pl.BlockSpec((kept, TILE, count * outer), lambda i: (0, 0, 0)),
        out_shape=jax.ShapeDtypeStruct((kept, TILE, count * outer), jnp.bfloat16),
        scratch_shapes=[
            pltpu.VMEM((outer, (frame_count + SUB - 1) // SUB * SUB, LANES), jnp.float32),
            pltpu.VMEM((count * outer, LANES), jnp.float32),
            pltpu.VMEM((count * outer // LANES, kept * TILE, LANES), jnp.float32),
        ],
        compiler_params=pltpu.CompilerParams(
            dimension_semantics=("arbitrary",), vmem_limit_bytes=48 * 2**20
        ),
    )(voltages, *fixed)


def correlate_kernel(
    n_stn, n_chan, count, spec_ref, mask_ref, out_ref, got, pair, mine,
    own_sem, send_sem, recv_sem, back_own, back_send, back_recv,
):
    grp = lax.axis_index("grp")
    stn = lax.axis_index("stn")
    chan = lax.axis_index("chan")
    reach = out_ref.shape[0]
    steps = got.shape[0]
    sub_groups = mask_ref.shape[0]
    block = TILE // 2 * n_chan
    across = LANES // block
    me = stn * n_chan + chan
    turns = [(a, b) for a in range(n_stn) for b in range(n_chan) if (a, b) != (0, 0)]

    def partner(turn):
        return lax.rem(stn + turn[0], n_stn), lax.rem(chan + turn[1], n_chan)

    def first_row(s, c):
        return (c * n_stn + s) * steps

    barrier = pltpu.get_barrier_semaphore()
    for turn in turns:
        s, c = partner(turn)
        pl.semaphore_signal(
            barrier, inc=1, device_id=(grp, s, c), device_id_type=pl.DeviceIdType.MESH
        )
    pl.semaphore_wait(barrier, len(turns))

    def own_copy(step):
        return pltpu.make_async_copy(
            spec_ref.at[first_row(stn, chan) + step], got.at[step, me], own_sem.at[step]
        )

    def outgoing(n, step):
        s, c = partner(turns[n])
        return pltpu.make_async_remote_copy(
            src_ref=spec_ref.at[first_row(s, c) + step],
            dst_ref=got.at[step, me],
            send_sem=send_sem.at[n, step],
            recv_sem=recv_sem.at[n, step],
            device_id=(grp, s, c),
            device_id_type=pl.DeviceIdType.MESH,
        )

    groups_here = steps * sub_groups

    def places(step):
        return pl.ds(step * sub_groups, sub_groups), pl.ds(
            stn * groups_here + step * sub_groups, sub_groups
        )

    def back_own_copy(step):
        src, dst = places(step)
        return pltpu.make_async_copy(mine.at[stn, :, src], out_ref.at[:, dst], back_own.at[step])

    def going_back(n, step):
        src, dst = places(step)
        s = lax.rem(stn + n, n_stn)
        return pltpu.make_async_remote_copy(
            src_ref=mine.at[s, :, src],
            dst_ref=out_ref.at[:, dst],
            send_sem=back_send.at[n - 1, step],
            recv_sem=back_recv.at[n - 1, step],
            device_id=(grp, s, chan),
            device_id_type=pl.DeviceIdType.MESH,
        )

    order = sorted(range(len(turns)), key=lambda n: -turns[n][0] % n_stn == 0)
    for step in range(steps):
        own_copy(step).start()
        for n in order:
            outgoing(n, step).start()

    scale = 1.0 / (count * AVG)
    n_rows = n_stn * n_chan * SUB
    lane_part = lax.broadcasted_iota(jnp.int32, (SUB, LANES), 1) // block

    def one_step(step, carry):
        own_copy(step).wait()
        for n in range(len(turns)):
            outgoing(n, step).wait_recv()
        both = got[step].astype(jnp.float32)
        width = both.shape[2]
        rows = jnp.concatenate(
            [both[:, :SUB, :].reshape(n_rows, width), both[:, SUB:, :].reshape(n_rows, width)], axis=0
        ).astype(jnp.bfloat16)
        for g in range(sub_groups):
            chosen = rows.reshape(2 * n_rows // TILE, TILE, width) * mask_ref[g][None]
            product = rows_by_rows(chosen.reshape(2 * n_rows, width), rows)
            pair[g, 0] = (product[:n_rows, :n_rows] + product[n_rows:, n_rows:]) * scale
            pair[g, 1] = (product[n_rows:, :n_rows] - product[:n_rows, n_rows:]) * scale
            for b in range(n_stn):
                slabs = [
                    [pair[g, part, pl.ds(b * block + e, SUB, stride=across), :] for e in range(across)]
                    for part in range(2)
                ]
                for d in range(reach):
                    other = (b + d) % n_stn
                    tiles = []
                    for part in range(2):
                        flat = None
                        for e in range(across):
                            shift = (e - other) % across * block
                            moved = pltpu.roll(slabs[part][e], shift, 1) if shift else slabs[part][e]
                            flat = moved if flat is None else jnp.where(lane_part == e, moved, flat)
                        tiles.append(flat)
                    mine[b, d, step * sub_groups + g] = jnp.concatenate(tiles, axis=0).astype(
                        jnp.bfloat16
                    )
        back_own_copy(step).start()
        for n in range(1, n_stn):
            going_back(n, step).start()
        return carry

    lax.fori_loop(0, steps, one_step, 0)

    for step in range(steps):
        back_own_copy(step).wait()
        for n in range(len(turns)):
            outgoing(n, step).wait_send()
        for n in range(1, n_stn):
            going_back(n, step).wait()


def correlate_all(spectra, n_stn, n_chan, count):
    kept, tile, width = spectra.shape
    outer = width // count
    steps = kept // (n_stn * n_chan)
    sub_groups = outer // AVG
    reach = n_stn // 2 + 1
    peers = n_stn * n_chan - 1
    groups = kept // n_chan * sub_groups
    mask = (np.arange(width) % outer // AVG)[None, :] == np.arange(sub_groups)[:, None]
    mask = jnp.asarray(
        np.broadcast_to(mask[:, None, :], (sub_groups, TILE, width)).astype(jnp.bfloat16)
    )
    vmem = pl.BlockSpec(memory_space=pltpu.VMEM)
    return pl.pallas_call(
        functools.partial(correlate_kernel, n_stn, n_chan, count),
        in_specs=[vmem, vmem],
        out_specs=vmem,
        out_shape=jax.ShapeDtypeStruct((reach, groups, TILE, LANES), jnp.bfloat16),
        scratch_shapes=[
            pltpu.VMEM((steps, n_stn * n_chan, TILE, width), jnp.bfloat16),
            pltpu.VMEM((sub_groups, 2, LANES, LANES), jnp.float32),
            pltpu.VMEM((n_stn, reach, steps * sub_groups, TILE, LANES), jnp.bfloat16),
            pltpu.SemaphoreType.DMA((steps,)),
            pltpu.SemaphoreType.DMA((peers, steps)),
            pltpu.SemaphoreType.DMA((peers, steps)),
            pltpu.SemaphoreType.DMA((steps,)),
            pltpu.SemaphoreType.DMA((n_stn - 1, steps)),
            pltpu.SemaphoreType.DMA((n_stn - 1, steps)),
        ],
        compiler_params=pltpu.CompilerParams(
            collective_id=0, has_side_effects=True, vmem_limit_bytes=48 * 2**20
        ),
    )(spectra, mask)


def local(voltages, taps):
    inputs_here, frame_count, frame_len = voltages.shape
    count = frame_count - taps.shape[0] + 1
    n_stn, n_chan = lax.axis_size("stn"), lax.axis_size("chan")
    outer = frame_len // LANES
    fits = (
        inputs_here == SUB
        and inputs_here * n_stn * n_chan == LANES
        and frame_len % (LANES * AVG) == 0
        and LANES % outer == 0
        and count % (2 * LANES // outer) == 0
        and count % TILE == 0
        and frame_len // 2 // outer % (n_stn * n_chan) == 0
        and (inputs_here * n_chan) ** 2 == SUB * LANES
    )
    if not fits:
        return general(voltages, taps)
    tiles = correlate_all(local_spectra(voltages, taps), n_stn, n_chan, count)
    reach, groups = tiles.shape[:2]
    return tiles.reshape(1, reach, groups, 2, (inputs_here * n_chan) ** 2)


def solution(mesh):
    placed = (P(("grp", "stn", "chan"), None, None), P())
    return jax.shard_map(
        local,
        mesh=mesh,
        in_specs=placed,
        out_specs=P(("grp", "stn"), None, "chan", None, None),
        check_vma=False,
    )
```

```python
import functools
import math

import jax
import jax.numpy as jnp
import numpy as np
from jax import lax
from jax.experimental import pallas as pl
from jax.experimental.pallas import tpu as pltpu
from jax.sharding import PartitionSpec as P

AVG = 16


def from_behind(shard, axis, by):
    size = lax.axis_size(axis)
    return lax.ppermute(shard, axis, [(i, (i + by) % size) for i in range(size)])


def angle_table(rows, cols, modulus):
    product = (
        jnp.arange(rows, dtype=jnp.int32)[:, None]
        * jnp.arange(cols, dtype=jnp.int32)[None, :]
        % modulus
    )
    return 2.0 * math.pi / modulus * product.astype(jnp.float32)


def transform(weighted):
    rows_total = weighted.shape[0] * weighted.shape[1]
    frame_len = weighted.shape[2]
    inner = 128
    outer = frame_len // inner
    kept = frame_len // 2 // inner
    highest = lax.Precision.HIGHEST
    samples = weighted.reshape(rows_total, inner, outer)
    first = angle_table(inner, inner, inner)
    first_real = jnp.einsum("rqp,qk->rpk", samples, jnp.cos(first), precision=highest)
    first_imag = -jnp.einsum("rqp,qk->rpk", samples, jnp.sin(first), precision=highest)
    twist = angle_table(outer, inner, frame_len)
    twist_cos = jnp.cos(twist)
    twist_sin = jnp.sin(twist)
    second_real = first_real * twist_cos + first_imag * twist_sin
    second_imag = first_imag * twist_cos - first_real * twist_sin
    third = angle_table(outer, kept, outer)
    third_cos = jnp.cos(third)
    third_sin = jnp.sin(third)
    out_real = jnp.einsum("rpk,pm->rmk", second_real, third_cos, precision=highest) + jnp.einsum(
        "rpk,pm->rmk", second_imag, third_sin, precision=highest
    )
    out_imag = jnp.einsum("rpk,pm->rmk", second_imag, third_cos, precision=highest) - jnp.einsum(
        "rpk,pm->rmk", second_real, third_sin, precision=highest
    )
    scale = frame_len ** (-0.5)
    return (
        out_real.reshape(rows_total, kept * inner) * scale,
        out_imag.reshape(rows_total, kept * inner) * scale,
    )


def general(voltages, taps):
    inputs_here, frames, frame_len = voltages.shape
    tap_count = taps.shape[0]
    spectra_count = frames - tap_count + 1
    channels = frame_len // 2
    weighted = taps[0] * voltages[:, 0:spectra_count, :].astype(jnp.float32)
    for tap_index in range(1, tap_count):
        weighted = weighted + taps[tap_index] * voltages[
            :, tap_index : tap_index + spectra_count, :
        ].astype(jnp.float32)
    out_real, out_imag = transform(weighted)
    spectra = (
        jnp.stack([out_real, out_imag])
        .reshape(2, inputs_here, spectra_count, channels)
        .astype(jnp.bfloat16)
    )
    turned = lax.all_to_all(spectra, "chan", split_axis=3, concat_axis=1, tiled=True)
    block_inputs = turned.shape[1]
    chan_here = turned.shape[3]
    groups = chan_here // AVG
    scale = 1.0 / (spectra_count * AVG)
    half = lax.axis_size("stn") // 2
    reach = half + 1
    block = turned.reshape(2, block_inputs, spectra_count, groups, AVG)
    block = block.transpose(3, 0, 1, 2, 4).reshape(groups, 2 * block_inputs, spectra_count * AVG)

    def correlate(own, other):
        product = jnp.einsum("gak,gck->gac", own, other, preferred_element_type=jnp.float32)
        real_vis = (
            product[:, :block_inputs, :block_inputs] + product[:, block_inputs:, block_inputs:]
        )
        imag_vis = (
            product[:, block_inputs:, :block_inputs] - product[:, :block_inputs, block_inputs:]
        )
        both = jnp.stack([real_vis, imag_vis], axis=1).reshape(
            groups, 2, block_inputs * block_inputs
        )
        return (both * scale).astype(jnp.bfloat16)

    tiles = jnp.zeros((reach, groups, 2, block_inputs * block_inputs), jnp.bfloat16)
    tiles = tiles.at[0].set(correlate(block, block))

    def advance(distance, carry):
        moving, stack_now = carry
        moving = from_behind(moving, "stn", -1)
        stack_now = lax.dynamic_update_index_in_dim(
            stack_now, correlate(block, moving), distance, 0
        )
        return (moving, stack_now)

    moved, tiles = lax.fori_loop(1, reach, advance, (block, tiles))
    return tiles[None]


LANES = 128
SUB = 8
TILE = 16


def halves(table):
    high = table.astype(jnp.bfloat16)
    low = (table - high.astype(np.float64)).astype(jnp.bfloat16)
    return high, low


def fourier_tables(frame_len):
    outer = frame_len // LANES
    kept = frame_len // 2 // outer
    high_digit = np.arange(outer)
    lane = np.arange(LANES)
    first = 2.0 * np.pi / outer * (np.outer(high_digit, high_digit) % outer)
    first = np.concatenate([np.cos(first), -np.sin(first)], axis=0)
    high, low = halves(first)
    first = np.concatenate([high, low, high], axis=1)
    twist = 2.0 * np.pi / frame_len * (np.outer(high_digit, lane) % frame_len)
    last = 2.0 * np.pi / LANES * (np.outer(np.arange(kept), lane) % LANES)
    cos, sin = np.cos(last), np.sin(last)
    last = np.concatenate(
        [np.concatenate([cos, sin], axis=1), np.concatenate([-sin, cos], axis=1)], axis=0
    )
    high, low = halves(last * frame_len ** (-0.5))
    last = np.stack([high, low])
    return first, np.stack([np.cos(twist), np.sin(twist)]).astype(np.float32), last


def rows_by_rows(left, right):
    return lax.dot_general(
        left, right, (((1,), (1,)), ((), ())), preferred_element_type=jnp.float32
    )


def split(values):
    high = values.astype(jnp.bfloat16)
    return high, (values - high.astype(jnp.float32)).astype(jnp.bfloat16)


def fused_kernel(
    n_stn, n_chan, v_ref, taps_ref, first_ref, twist_ref, last_ref, mask_ref, out_ref,
    weighted, held, spec, got, pair, mine,
    own_sem, send_sem, recv_sem, back_own, back_send, back_recv,
):
    grp = lax.axis_index("grp")
    stn = lax.axis_index("stn")
    chan = lax.axis_index("chan")
    reach = out_ref.shape[0]
    chunks, _, steps, _, width = got.shape
    outer = v_ref.shape[2] // LANES
    kept = spec.shape[1]
    tap_count = taps_ref.shape[0]
    count = v_ref.shape[0] - tap_count + 1
    per_chunk = count // chunks
    sub_groups = mask_ref.shape[0]
    block = TILE // 2 * n_chan
    across = LANES // block
    me = stn * n_chan + chan
    turns = [(a, b) for a in range(n_stn) for b in range(n_chan) if (a, b) != (0, 0)]

    def partner(turn):
        return lax.rem(stn + turn[0], n_stn), lax.rem(chan + turn[1], n_chan)

    def first_row(s, c):
        return (c * n_stn + s) * steps

    barrier = pltpu.get_barrier_semaphore()
    for turn in turns:
        s, c = partner(turn)
        pl.semaphore_signal(
            barrier, inc=1, device_id=(grp, s, c), device_id_type=pl.DeviceIdType.MESH
        )
    pl.semaphore_wait(barrier, len(turns))

    def own_copy(chunk):
        return pltpu.make_async_copy(
            spec.at[chunk, pl.ds(first_row(stn, chan), steps)], got.at[chunk, me], own_sem.at[chunk]
        )

    def outgoing(n, chunk):
        s, c = partner(turns[n])
        return pltpu.make_async_remote_copy(
            src_ref=spec.at[chunk, pl.ds(first_row(s, c), steps)],
            dst_ref=got.at[chunk, me],
            send_sem=send_sem.at[n, chunk],
            recv_sem=recv_sem.at[n, chunk],
            device_id=(grp, s, c),
            device_id_type=pl.DeviceIdType.MESH,
        )

    groups_here = steps * sub_groups

    def places(step):
        return pl.ds(step * sub_groups, sub_groups), pl.ds(
            stn * groups_here + step * sub_groups, sub_groups
        )

    def back_own_copy(step):
        src, dst = places(step)
        return pltpu.make_async_copy(mine.at[stn, :, src], out_ref.at[:, dst], back_own.at[step])

    def going_back(n, step):
        src, dst = places(step)
        s = lax.rem(stn + n, n_stn)
        return pltpu.make_async_remote_copy(
            src_ref=mine.at[s, :, src],
            dst_ref=out_ref.at[:, dst],
            send_sem=back_send.at[n - 1, step],
            recv_sem=back_recv.at[n - 1, step],
            device_id=(grp, s, chan),
            device_id_type=pl.DeviceIdType.MESH,
        )

    order = sorted(range(len(turns)), key=lambda n: turns[n][0] == 0)

    def one_chunk(chunk, carry):
        def filter_tile(tile, inner):
            lanes = pl.ds(pl.multiple_of(tile * LANES, LANES), LANES)
            frames = [
                v_ref[chunk * per_chunk + t, :, lanes].astype(jnp.float32)
                for t in range(per_chunk + tap_count - 1)
            ]
            totals = [None] * per_chunk
            for t in range(tap_count):
                tap = jnp.broadcast_to(taps_ref[t : t + 1, lanes], (SUB, LANES))
                for s in range(per_chunk):
                    term = tap * frames[s + t]
                    totals[s] = term if t == 0 else totals[s] + term
            for s in range(per_chunk):
                weighted[pl.ds(s * SUB * outer + tile, SUB, stride=outer), :] = totals[s]
            return inner

        lax.fori_loop(0, outer, filter_tile, 0, unroll=2)

        def one_input(i, inner):
            parts = []
            for s in range(0, per_chunk, 2):
                samples = jnp.concatenate(
                    [
                        weighted[pl.ds(pl.multiple_of(((s + k) * SUB + i) * outer, outer), outer), :]
                        for k in range(2)
                    ],
                    axis=1,
                )
                high, low = split(samples)
                y = jnp.dot(
                    first_ref[...],
                    jnp.concatenate([high, high, low], axis=0),
                    preferred_element_type=jnp.float32,
                )
                for k in range(2):
                    real = y[:outer, k * LANES : (k + 1) * LANES]
                    imag = y[outer:, k * LANES : (k + 1) * LANES]
                    parts.append(
                        jnp.concatenate(
                            [
                                real * twist_ref[0] + imag * twist_ref[1],
                                imag * twist_ref[0] - real * twist_ref[1],
                            ],
                            axis=1,
                        )
                    )
            high, low = split(jnp.concatenate(parts, axis=0))
            result = (
                rows_by_rows(last_ref[0], high)
                + rows_by_rows(last_ref[1], high)
                + rows_by_rows(last_ref[0], low)
            )
            for part in range(2):
                for k in range(width // LANES):
                    held[k, pl.ds(part * SUB + i, kept, stride=TILE), :] = result[
                        part * kept : (part + 1) * kept, k * LANES : (k + 1) * LANES
                    ]
            return inner

        lax.fori_loop(0, SUB, one_input, 0, unroll=2)
        for k in range(width // LANES):
            spec[chunk, :, :, k * LANES : (k + 1) * LANES] = (
                held[k].reshape(kept, TILE, LANES).astype(jnp.bfloat16)
            )
        own_copy(chunk).start()
        for n in order:
            outgoing(n, chunk).start()
        return carry

    lax.fori_loop(0, chunks, one_chunk, 0)

    for chunk in range(chunks):
        own_copy(chunk).wait()
        for n in range(len(turns)):
            outgoing(n, chunk).wait_recv()

    scale = 1.0 / (count * AVG)
    n_rows = n_stn * n_chan * SUB
    lane_part = lax.broadcasted_iota(jnp.int32, (SUB, LANES), 1) // block

    def one_step(step, carry):
        columns = []
        for chunk in range(chunks):
            both = got[chunk, :, step].astype(jnp.float32)
            columns.append(
                jnp.concatenate(
                    [both[:, :SUB, :].reshape(n_rows, width), both[:, SUB:, :].reshape(n_rows, width)],
                    axis=0,
                ).astype(jnp.bfloat16)
            )
        rows = jnp.concatenate(columns, axis=1)
        total = chunks * width
        for g in range(sub_groups):
            chosen = rows.reshape(2 * n_rows // TILE, TILE, total) * mask_ref[g][None]
            product = rows_by_rows(chosen.reshape(2 * n_rows, total), rows)
            pair[g, 0] = (product[:n_rows, :n_rows] + product[n_rows:, n_rows:]) * scale
            pair[g, 1] = (product[n_rows:, :n_rows] - product[:n_rows, n_rows:]) * scale
            for b in range(n_stn):
                slabs = [
                    [pair[g, part, pl.ds(b * block + e, SUB, stride=across), :] for e in range(across)]
                    for part in range(2)
                ]
                for d in range(reach):
                    other = (b + d) % n_stn
                    tiles = []
                    for part in range(2):
                        flat = None
                        for e in range(across):
                            shift = (e - other) % across * block
                            moved = pltpu.roll(slabs[part][e], shift, 1) if shift else slabs[part][e]
                            flat = moved if flat is None else jnp.where(lane_part == e, moved, flat)
                        tiles.append(flat)
                    mine[b, d, step * sub_groups + g] = jnp.concatenate(tiles, axis=0).astype(
                        jnp.bfloat16
                    )
        back_own_copy(step).start()
        for n in range(1, n_stn):
            going_back(n, step).start()
        return carry

    lax.fori_loop(0, steps, one_step, 0)

    for chunk in range(chunks):
        for n in range(len(turns)):
            outgoing(n, chunk).wait_send()
    for step in range(steps):
        back_own_copy(step).wait()
        for n in range(1, n_stn):
            going_back(n, step).wait()


def fused(voltages, taps, n_stn, n_chan):
    inputs_here, frame_count, frame_len = voltages.shape
    count = frame_count - taps.shape[0] + 1
    outer = frame_len // LANES
    kept = frame_len // 2 // outer
    per_chunk = 2 * LANES // outer
    chunks = count // per_chunk
    width = per_chunk * outer
    peers = n_stn * n_chan - 1
    steps = kept // (n_stn * n_chan)
    sub_groups = outer // AVG
    reach = n_stn // 2 + 1
    groups = kept // n_chan * sub_groups
    mask = (np.arange(count * outer) % outer // AVG)[None, :] == np.arange(sub_groups)[:, None]
    mask = np.broadcast_to(mask[:, None, :], (sub_groups, TILE, count * outer)).astype(jnp.bfloat16)
    tables = [jnp.asarray(t) for t in (*fourier_tables(frame_len), mask)]
    vmem = pl.BlockSpec(memory_space=pltpu.VMEM)
    return pl.pallas_call(
        functools.partial(fused_kernel, n_stn, n_chan),
        in_specs=[vmem] * 6,
        out_specs=vmem,
        out_shape=jax.ShapeDtypeStruct((reach, groups, TILE, LANES), jnp.bfloat16),
        scratch_shapes=[
            pltpu.VMEM((per_chunk * inputs_here * outer, LANES), jnp.float32),
            pltpu.VMEM((width // LANES, kept * TILE, LANES), jnp.float32),
            pltpu.VMEM((chunks, kept, TILE, width), jnp.bfloat16),
            pltpu.VMEM((chunks, n_stn * n_chan, steps, TILE, width), jnp.bfloat16),
            pltpu.VMEM((sub_groups, 2, LANES, LANES), jnp.float32),
            pltpu.VMEM((n_stn, reach, steps * sub_groups, TILE, LANES), jnp.bfloat16),
            pltpu.SemaphoreType.DMA((chunks,)),
            pltpu.SemaphoreType.DMA((peers, chunks)),
            pltpu.SemaphoreType.DMA((peers, chunks)),
            pltpu.SemaphoreType.DMA((steps,)),
            pltpu.SemaphoreType.DMA((n_stn - 1, steps)),
            pltpu.SemaphoreType.DMA((n_stn - 1, steps)),
        ],
        compiler_params=pltpu.CompilerParams(
            collective_id=0, has_side_effects=True, vmem_limit_bytes=48 * 2**20
        ),
    )(jnp.transpose(voltages, (1, 0, 2)), taps, *tables)


def local(voltages, taps):
    inputs_here, frame_count, frame_len = voltages.shape
    count = frame_count - taps.shape[0] + 1
    n_stn, n_chan = lax.axis_size("stn"), lax.axis_size("chan")
    outer = frame_len // LANES
    fits = (
        inputs_here == SUB
        and inputs_here * n_stn * n_chan == LANES
        and frame_len % (LANES * AVG) == 0
        and LANES % outer == 0
        and count % (2 * LANES // outer) == 0
        and count % TILE == 0
        and frame_len // 2 // outer % (n_stn * n_chan) == 0
        and (inputs_here * n_chan) ** 2 == SUB * LANES
    )
    if not fits:
        return general(voltages, taps)
    tiles = fused(voltages, taps, n_stn, n_chan)
    reach, groups = tiles.shape[:2]
    return tiles.reshape(1, reach, groups, 2, (inputs_here * n_chan) ** 2)


def solution(mesh):
    placed = (P(("grp", "stn", "chan"), None, None), P())
    return jax.shard_map(
        local,
        mesh=mesh,
        in_specs=placed,
        out_specs=P(("grp", "stn"), None, "chan", None, None),
        check_vma=False,
    )
```

```python
import functools
import math

import jax
import jax.numpy as jnp
import numpy as np
from jax import lax
from jax.experimental import pallas as pl
from jax.experimental.pallas import tpu as pltpu
from jax.sharding import PartitionSpec as P

AVG = 16


def from_behind(shard, axis, by):
    size = lax.axis_size(axis)
    return lax.ppermute(shard, axis, [(i, (i + by) % size) for i in range(size)])


def angle_table(rows, cols, modulus):
    product = (
        jnp.arange(rows, dtype=jnp.int32)[:, None]
        * jnp.arange(cols, dtype=jnp.int32)[None, :]
        % modulus
    )
    return 2.0 * math.pi / modulus * product.astype(jnp.float32)


def transform(weighted):
    rows_total = weighted.shape[0] * weighted.shape[1]
    frame_len = weighted.shape[2]
    inner = 128
    outer = frame_len // inner
    kept = frame_len // 2 // inner
    highest = lax.Precision.HIGHEST
    samples = weighted.reshape(rows_total, inner, outer)
    first = angle_table(inner, inner, inner)
    first_real = jnp.einsum("rqp,qk->rpk", samples, jnp.cos(first), precision=highest)
    first_imag = -jnp.einsum("rqp,qk->rpk", samples, jnp.sin(first), precision=highest)
    twist = angle_table(outer, inner, frame_len)
    twist_cos = jnp.cos(twist)
    twist_sin = jnp.sin(twist)
    second_real = first_real * twist_cos + first_imag * twist_sin
    second_imag = first_imag * twist_cos - first_real * twist_sin
    third = angle_table(outer, kept, outer)
    third_cos = jnp.cos(third)
    third_sin = jnp.sin(third)
    out_real = jnp.einsum("rpk,pm->rmk", second_real, third_cos, precision=highest) + jnp.einsum(
        "rpk,pm->rmk", second_imag, third_sin, precision=highest
    )
    out_imag = jnp.einsum("rpk,pm->rmk", second_imag, third_cos, precision=highest) - jnp.einsum(
        "rpk,pm->rmk", second_real, third_sin, precision=highest
    )
    scale = frame_len ** (-0.5)
    return (
        out_real.reshape(rows_total, kept * inner) * scale,
        out_imag.reshape(rows_total, kept * inner) * scale,
    )


def general(voltages, taps):
    inputs_here, frames, frame_len = voltages.shape
    tap_count = taps.shape[0]
    spectra_count = frames - tap_count + 1
    channels = frame_len // 2
    weighted = taps[0] * voltages[:, 0:spectra_count, :].astype(jnp.float32)
    for tap_index in range(1, tap_count):
        weighted = weighted + taps[tap_index] * voltages[
            :, tap_index : tap_index + spectra_count, :
        ].astype(jnp.float32)
    out_real, out_imag = transform(weighted)
    spectra = (
        jnp.stack([out_real, out_imag])
        .reshape(2, inputs_here, spectra_count, channels)
        .astype(jnp.bfloat16)
    )
    turned = lax.all_to_all(spectra, "chan", split_axis=3, concat_axis=1, tiled=True)
    block_inputs = turned.shape[1]
    chan_here = turned.shape[3]
    groups = chan_here // AVG
    scale = 1.0 / (spectra_count * AVG)
    half = lax.axis_size("stn") // 2
    reach = half + 1
    block = turned.reshape(2, block_inputs, spectra_count, groups, AVG)
    block = block.transpose(3, 0, 1, 2, 4).reshape(groups, 2 * block_inputs, spectra_count * AVG)

    def correlate(own, other):
        product = jnp.einsum("gak,gck->gac", own, other, preferred_element_type=jnp.float32)
        real_vis = (
            product[:, :block_inputs, :block_inputs] + product[:, block_inputs:, block_inputs:]
        )
        imag_vis = (
            product[:, block_inputs:, :block_inputs] - product[:, :block_inputs, block_inputs:]
        )
        both = jnp.stack([real_vis, imag_vis], axis=1).reshape(
            groups, 2, block_inputs * block_inputs
        )
        return (both * scale).astype(jnp.bfloat16)

    tiles = jnp.zeros((reach, groups, 2, block_inputs * block_inputs), jnp.bfloat16)
    tiles = tiles.at[0].set(correlate(block, block))

    def advance(distance, carry):
        moving, stack_now = carry
        moving = from_behind(moving, "stn", -1)
        stack_now = lax.dynamic_update_index_in_dim(
            stack_now, correlate(block, moving), distance, 0
        )
        return (moving, stack_now)

    moved, tiles = lax.fori_loop(1, reach, advance, (block, tiles))
    return tiles[None]


LANES = 128
SUB = 8
TILE = 16


def halves(table):
    high = table.astype(jnp.bfloat16)
    low = (table - high.astype(np.float64)).astype(jnp.bfloat16)
    return high, low


def fourier_tables(frame_len):
    outer = frame_len // LANES
    kept = frame_len // 2 // outer
    high_digit = np.arange(outer)
    lane = np.arange(LANES)
    first = 2.0 * np.pi / outer * (np.outer(high_digit, high_digit) % outer)
    first = np.concatenate([np.cos(first), -np.sin(first)], axis=0)
    high, low = halves(first)
    first = np.concatenate([high, low, high], axis=1)
    twist = 2.0 * np.pi / frame_len * (np.outer(high_digit, lane) % frame_len)
    last = 2.0 * np.pi / LANES * (np.outer(np.arange(kept), lane) % LANES)
    cos, sin = np.cos(last), np.sin(last)
    last = np.concatenate(
        [np.concatenate([cos, sin], axis=1), np.concatenate([-sin, cos], axis=1)], axis=0
    )
    high, low = halves(last * frame_len ** (-0.5))
    last = np.stack([high, low])
    return first, np.stack([np.cos(twist), np.sin(twist)]).astype(np.float32), last


def rows_by_rows(left, right):
    return lax.dot_general(
        left, right, (((1,), (1,)), ((), ())), preferred_element_type=jnp.float32
    )


def split(values):
    high = values.astype(jnp.bfloat16)
    return high, (values - high.astype(jnp.float32)).astype(jnp.bfloat16)


def fused_kernel(
    n_stn, n_chan, v_hbm, taps_hbm, first_hbm, twist_hbm, last_hbm, mask_hbm, out_ref,
    v_ref, taps_ref, first_ref, twist_ref, last_ref, mask_ref, in_sem, weighted, held, spec, got, pair, mine,
    own_sem, send_sem, recv_sem, back_own, back_send, back_recv,
):
    grp = lax.axis_index("grp")
    stn = lax.axis_index("stn")
    chan = lax.axis_index("chan")
    reach = out_ref.shape[0]
    chunks, _, steps, _, width = got.shape
    outer = v_ref.shape[2] // LANES
    kept = spec.shape[1]
    tap_count = taps_ref.shape[0]
    count = v_ref.shape[0] - tap_count + 1
    per_chunk = count // chunks
    sub_groups = mask_ref.shape[0]
    block = TILE // 2 * n_chan
    across = LANES // block
    me = stn * n_chan + chan
    turns = [(a, b) for a in range(n_stn) for b in range(n_chan) if (a, b) != (0, 0)]

    def partner(turn):
        return lax.rem(stn + turn[0], n_stn), lax.rem(chan + turn[1], n_chan)

    def first_row(s, c):
        return (c * n_stn + s) * steps

    ahead = per_chunk + tap_count - 1
    loads = [
        pltpu.make_async_copy(v_hbm.at[pl.ds(0, ahead)], v_ref.at[pl.ds(0, ahead)], in_sem.at[0]),
        pltpu.make_async_copy(taps_hbm, taps_ref, in_sem.at[1]),
        pltpu.make_async_copy(first_hbm, first_ref, in_sem.at[2]),
        pltpu.make_async_copy(twist_hbm, twist_ref, in_sem.at[3]),
        pltpu.make_async_copy(last_hbm, last_ref, in_sem.at[4]),
    ]
    rest = pl.ds(ahead, v_ref.shape[0] - ahead)
    later = pltpu.make_async_copy(v_hbm.at[rest], v_ref.at[rest], in_sem.at[5])
    last_load = pltpu.make_async_copy(mask_hbm, mask_ref, in_sem.at[6])
    for copy in [*loads, later, last_load]:
        copy.start()

    barrier = pltpu.get_barrier_semaphore()
    for turn in turns:
        s, c = partner(turn)
        pl.semaphore_signal(
            barrier, inc=1, device_id=(grp, s, c), device_id_type=pl.DeviceIdType.MESH
        )
    pl.semaphore_wait(barrier, len(turns))

    def own_copy(chunk):
        return pltpu.make_async_copy(
            spec.at[chunk, pl.ds(first_row(stn, chan), steps)], got.at[chunk, me], own_sem.at[chunk]
        )

    def outgoing(n, chunk):
        s, c = partner(turns[n])
        return pltpu.make_async_remote_copy(
            src_ref=spec.at[chunk, pl.ds(first_row(s, c), steps)],
            dst_ref=got.at[chunk, me],
            send_sem=send_sem.at[n, chunk],
            recv_sem=recv_sem.at[n, chunk],
            device_id=(grp, s, c),
            device_id_type=pl.DeviceIdType.MESH,
        )

    groups_here = steps * sub_groups

    def places(step):
        return pl.ds(step * sub_groups, sub_groups), pl.ds(
            stn * groups_here + step * sub_groups, sub_groups
        )

    def back_own_copy(step):
        src, dst = places(step)
        return pltpu.make_async_copy(mine.at[stn, :, src], out_ref.at[:, dst], back_own.at[step])

    def going_back(n, step):
        src, dst = places(step)
        s = lax.rem(stn + n, n_stn)
        return pltpu.make_async_remote_copy(
            src_ref=mine.at[s, :, src],
            dst_ref=out_ref.at[:, dst],
            send_sem=back_send.at[n - 1, step],
            recv_sem=back_recv.at[n - 1, step],
            device_id=(grp, s, chan),
            device_id_type=pl.DeviceIdType.MESH,
        )

    order = sorted(range(len(turns)), key=lambda n: turns[n][0] == 0)

    def one_chunk(chunk, carry):
        @pl.when(chunk == 1)
        def _():
            later.wait()

        def filter_tile(tile, inner):
            lanes = pl.ds(pl.multiple_of(tile * LANES, LANES), LANES)
            frames = [
                v_ref[chunk * per_chunk + t, :, lanes].astype(jnp.float32)
                for t in range(per_chunk + tap_count - 1)
            ]
            totals = [None] * per_chunk
            for t in range(tap_count):
                tap = jnp.broadcast_to(taps_ref[t : t + 1, lanes], (SUB, LANES))
                for s in range(per_chunk):
                    term = tap * frames[s + t]
                    totals[s] = term if t == 0 else totals[s] + term
            for s in range(per_chunk):
                weighted[pl.ds(s * SUB * outer + tile, SUB, stride=outer), :] = totals[s]
            return inner

        lax.fori_loop(0, outer, filter_tile, 0, unroll=2)

        def one_input(i, inner):
            parts = []
            for s in range(0, per_chunk, 2):
                samples = jnp.concatenate(
                    [
                        weighted[pl.ds(pl.multiple_of(((s + k) * SUB + i) * outer, outer), outer), :]
                        for k in range(2)
                    ],
                    axis=1,
                )
                high, low = split(samples)
                y = jnp.dot(
                    first_ref[...],
                    jnp.concatenate([high, high, low], axis=0),
                    preferred_element_type=jnp.float32,
                )
                for k in range(2):
                    real = y[:outer, k * LANES : (k + 1) * LANES]
                    imag = y[outer:, k * LANES : (k + 1) * LANES]
                    parts.append(
                        jnp.concatenate(
                            [
                                real * twist_ref[0] + imag * twist_ref[1],
                                imag * twist_ref[0] - real * twist_ref[1],
                            ],
                            axis=1,
                        )
                    )
            high, low = split(jnp.concatenate(parts, axis=0))
            result = (
                rows_by_rows(last_ref[0], high)
                + rows_by_rows(last_ref[1], high)
                + rows_by_rows(last_ref[0], low)
            )
            for part in range(2):
                for k in range(width // LANES):
                    held[k, pl.ds(part * SUB + i, kept, stride=TILE), :] = result[
                        part * kept : (part + 1) * kept, k * LANES : (k + 1) * LANES
                    ]
            return inner

        lax.fori_loop(0, SUB, one_input, 0, unroll=2)
        for k in range(width // LANES):
            spec[chunk, :, :, k * LANES : (k + 1) * LANES] = (
                held[k].reshape(kept, TILE, LANES).astype(jnp.bfloat16)
            )
        own_copy(chunk).start()
        for n in order:
            outgoing(n, chunk).start()
        return carry

    for copy in loads:
        copy.wait()
    lax.fori_loop(0, chunks, one_chunk, 0)
    last_load.wait()

    for chunk in range(chunks):
        own_copy(chunk).wait()
        for n in range(len(turns)):
            outgoing(n, chunk).wait_recv()

    scale = 1.0 / (count * AVG)
    n_rows = n_stn * n_chan * SUB
    lane_part = lax.broadcasted_iota(jnp.int32, (SUB, LANES), 1) // block

    def one_step(step, carry):
        columns = []
        for chunk in range(chunks):
            both = got[chunk, :, step].astype(jnp.float32)
            columns.append(
                jnp.concatenate(
                    [both[:, :SUB, :].reshape(n_rows, width), both[:, SUB:, :].reshape(n_rows, width)],
                    axis=0,
                ).astype(jnp.bfloat16)
            )
        rows = jnp.concatenate(columns, axis=1)
        total = chunks * width
        for g in range(sub_groups):
            chosen = rows.reshape(2 * n_rows // TILE, TILE, total) * mask_ref[g][None]
            product = rows_by_rows(chosen.reshape(2 * n_rows, total), rows)
            pair[g, 0] = (product[:n_rows, :n_rows] + product[n_rows:, n_rows:]) * scale
            pair[g, 1] = (product[n_rows:, :n_rows] - product[:n_rows, n_rows:]) * scale
            for b in range(n_stn):
                slabs = [
                    [pair[g, part, pl.ds(b * block + e, SUB, stride=across), :] for e in range(across)]
                    for part in range(2)
                ]
                for d in range(reach):
                    other = (b + d) % n_stn
                    tiles = []
                    for part in range(2):
                        flat = None
                        for e in range(across):
                            shift = (e - other) % across * block
                            moved = pltpu.roll(slabs[part][e], shift, 1) if shift else slabs[part][e]
                            flat = moved if flat is None else jnp.where(lane_part == e, moved, flat)
                        tiles.append(flat)
                    mine[b, d, step * sub_groups + g] = jnp.concatenate(tiles, axis=0).astype(
                        jnp.bfloat16
                    )
        back_own_copy(step).start()
        for n in range(1, n_stn):
            going_back(n, step).start()
        return carry

    lax.fori_loop(0, steps, one_step, 0)

    for chunk in range(chunks):
        for n in range(len(turns)):
            outgoing(n, chunk).wait_send()
    for step in range(steps):
        back_own_copy(step).wait()
        for n in range(1, n_stn):
            going_back(n, step).wait()


def fused(voltages, taps, n_stn, n_chan):
    inputs_here, frame_count, frame_len = voltages.shape
    count = frame_count - taps.shape[0] + 1
    outer = frame_len // LANES
    kept = frame_len // 2 // outer
    per_chunk = 2 * LANES // outer
    chunks = count // per_chunk
    width = per_chunk * outer
    peers = n_stn * n_chan - 1
    steps = kept // (n_stn * n_chan)
    sub_groups = outer // AVG
    reach = n_stn // 2 + 1
    groups = kept // n_chan * sub_groups
    mask = (np.arange(count * outer) % outer // AVG)[None, :] == np.arange(sub_groups)[:, None]
    mask = np.broadcast_to(mask[:, None, :], (sub_groups, TILE, count * outer)).astype(jnp.bfloat16)
    tables = [jnp.asarray(t) for t in (*fourier_tables(frame_len), mask)]
    frames_first = jnp.transpose(voltages, (1, 0, 2))
    vmem = pl.BlockSpec(memory_space=pltpu.VMEM)
    return pl.pallas_call(
        functools.partial(fused_kernel, n_stn, n_chan),
        in_specs=[pl.BlockSpec(memory_space=pltpu.HBM)] * (2 + len(tables)),
        out_specs=vmem,
        out_shape=jax.ShapeDtypeStruct((reach, groups, TILE, LANES), jnp.bfloat16),
        scratch_shapes=[pltpu.VMEM(a.shape, a.dtype) for a in (frames_first, taps, *tables)]
        + [
            pltpu.SemaphoreType.DMA((7,)),
            pltpu.VMEM((per_chunk * inputs_here * outer, LANES), jnp.float32),
            pltpu.VMEM((width // LANES, kept * TILE, LANES), jnp.float32),
            pltpu.VMEM((chunks, kept, TILE, width), jnp.bfloat16),
            pltpu.VMEM((chunks, n_stn * n_chan, steps, TILE, width), jnp.bfloat16),
            pltpu.VMEM((sub_groups, 2, LANES, LANES), jnp.float32),
            pltpu.VMEM((n_stn, reach, steps * sub_groups, TILE, LANES), jnp.bfloat16),
            pltpu.SemaphoreType.DMA((chunks,)),
            pltpu.SemaphoreType.DMA((peers, chunks)),
            pltpu.SemaphoreType.DMA((peers, chunks)),
            pltpu.SemaphoreType.DMA((steps,)),
            pltpu.SemaphoreType.DMA((n_stn - 1, steps)),
            pltpu.SemaphoreType.DMA((n_stn - 1, steps)),
        ],
        compiler_params=pltpu.CompilerParams(
            collective_id=0, has_side_effects=True, vmem_limit_bytes=48 * 2**20
        ),
    )(frames_first, taps, *tables)


def local(voltages, taps):
    inputs_here, frame_count, frame_len = voltages.shape
    count = frame_count - taps.shape[0] + 1
    n_stn, n_chan = lax.axis_size("stn"), lax.axis_size("chan")
    outer = frame_len // LANES
    fits = (
        inputs_here == SUB
        and inputs_here * n_stn * n_chan == LANES
        and frame_len % (LANES * AVG) == 0
        and LANES % outer == 0
        and count % (2 * LANES // outer) == 0
        and count % TILE == 0
        and count > 2 * LANES // outer
        and frame_len // 2 // outer % (n_stn * n_chan) == 0
        and (inputs_here * n_chan) ** 2 == SUB * LANES
    )
    if not fits:
        return general(voltages, taps)
    tiles = fused(voltages, taps, n_stn, n_chan)
    reach, groups = tiles.shape[:2]
    return tiles.reshape(1, reach, groups, 2, (inputs_here * n_chan) ** 2)


def solution(mesh):
    placed = (P(("grp", "stn", "chan"), None, None), P())
    return jax.shard_map(
        local,
        mesh=mesh,
        in_specs=placed,
        out_specs=P(("grp", "stn"), None, "chan", None, None),
        check_vma=False,
    )
```

```python
import functools
import math

import jax
import jax.numpy as jnp
import numpy as np
from jax import lax
from jax.experimental import pallas as pl
from jax.experimental.pallas import tpu as pltpu
from jax.sharding import PartitionSpec as P

AVG = 16


def from_behind(shard, axis, by):
    size = lax.axis_size(axis)
    return lax.ppermute(shard, axis, [(i, (i + by) % size) for i in range(size)])


def angle_table(rows, cols, modulus):
    product = (
        jnp.arange(rows, dtype=jnp.int32)[:, None]
        * jnp.arange(cols, dtype=jnp.int32)[None, :]
        % modulus
    )
    return 2.0 * math.pi / modulus * product.astype(jnp.float32)


def transform(weighted):
    rows_total = weighted.shape[0] * weighted.shape[1]
    frame_len = weighted.shape[2]
    inner = 128
    outer = frame_len // inner
    kept = frame_len // 2 // inner
    highest = lax.Precision.HIGHEST
    samples = weighted.reshape(rows_total, inner, outer)
    first = angle_table(inner, inner, inner)
    first_real = jnp.einsum("rqp,qk->rpk", samples, jnp.cos(first), precision=highest)
    first_imag = -jnp.einsum("rqp,qk->rpk", samples, jnp.sin(first), precision=highest)
    twist = angle_table(outer, inner, frame_len)
    twist_cos = jnp.cos(twist)
    twist_sin = jnp.sin(twist)
    second_real = first_real * twist_cos + first_imag * twist_sin
    second_imag = first_imag * twist_cos - first_real * twist_sin
    third = angle_table(outer, kept, outer)
    third_cos = jnp.cos(third)
    third_sin = jnp.sin(third)
    out_real = jnp.einsum("rpk,pm->rmk", second_real, third_cos, precision=highest) + jnp.einsum(
        "rpk,pm->rmk", second_imag, third_sin, precision=highest
    )
    out_imag = jnp.einsum("rpk,pm->rmk", second_imag, third_cos, precision=highest) - jnp.einsum(
        "rpk,pm->rmk", second_real, third_sin, precision=highest
    )
    scale = frame_len ** (-0.5)
    return (
        out_real.reshape(rows_total, kept * inner) * scale,
        out_imag.reshape(rows_total, kept * inner) * scale,
    )


def general(voltages, taps):
    inputs_here, frames, frame_len = voltages.shape
    tap_count = taps.shape[0]
    spectra_count = frames - tap_count + 1
    channels = frame_len // 2
    weighted = taps[0] * voltages[:, 0:spectra_count, :].astype(jnp.float32)
    for tap_index in range(1, tap_count):
        weighted = weighted + taps[tap_index] * voltages[
            :, tap_index : tap_index + spectra_count, :
        ].astype(jnp.float32)
    out_real, out_imag = transform(weighted)
    spectra = (
        jnp.stack([out_real, out_imag])
        .reshape(2, inputs_here, spectra_count, channels)
        .astype(jnp.bfloat16)
    )
    turned = lax.all_to_all(spectra, "chan", split_axis=3, concat_axis=1, tiled=True)
    block_inputs = turned.shape[1]
    chan_here = turned.shape[3]
    groups = chan_here // AVG
    scale = 1.0 / (spectra_count * AVG)
    half = lax.axis_size("stn") // 2
    reach = half + 1
    block = turned.reshape(2, block_inputs, spectra_count, groups, AVG)
    block = block.transpose(3, 0, 1, 2, 4).reshape(groups, 2 * block_inputs, spectra_count * AVG)

    def correlate(own, other):
        product = jnp.einsum("gak,gck->gac", own, other, preferred_element_type=jnp.float32)
        real_vis = (
            product[:, :block_inputs, :block_inputs] + product[:, block_inputs:, block_inputs:]
        )
        imag_vis = (
            product[:, block_inputs:, :block_inputs] - product[:, :block_inputs, block_inputs:]
        )
        both = jnp.stack([real_vis, imag_vis], axis=1).reshape(
            groups, 2, block_inputs * block_inputs
        )
        return (both * scale).astype(jnp.bfloat16)

    tiles = jnp.zeros((reach, groups, 2, block_inputs * block_inputs), jnp.bfloat16)
    tiles = tiles.at[0].set(correlate(block, block))

    def advance(distance, carry):
        moving, stack_now = carry
        moving = from_behind(moving, "stn", -1)
        stack_now = lax.dynamic_update_index_in_dim(
            stack_now, correlate(block, moving), distance, 0
        )
        return (moving, stack_now)

    moved, tiles = lax.fori_loop(1, reach, advance, (block, tiles))
    return tiles[None]


LANES = 128
SUB = 8
TILE = 16


def halves(table):
    high = table.astype(jnp.bfloat16)
    low = (table - high.astype(np.float64)).astype(jnp.bfloat16)
    return high, low


def fourier_tables(frame_len):
    outer = frame_len // LANES
    kept = frame_len // 2 // outer
    high_digit = np.arange(outer)
    lane = np.arange(LANES)
    first = 2.0 * np.pi / outer * (np.outer(high_digit, high_digit) % outer)
    first = np.concatenate([np.cos(first), -np.sin(first)], axis=0)
    high, low = halves(first)
    first = np.concatenate([high, low, high], axis=1)
    twist = 2.0 * np.pi / frame_len * (np.outer(high_digit, lane) % frame_len)
    last = 2.0 * np.pi / LANES * (np.outer(np.arange(kept), lane) % LANES)
    cos, sin = np.cos(last), np.sin(last)
    last = np.concatenate(
        [np.concatenate([cos, sin], axis=1), np.concatenate([-sin, cos], axis=1)], axis=0
    )
    high, low = halves(last * frame_len ** (-0.5))
    last = np.stack([high, low])
    return first, np.stack([np.cos(twist), np.sin(twist)]).astype(np.float32), last


def rows_by_rows(left, right):
    return lax.dot_general(
        left, right, (((1,), (1,)), ((), ())), preferred_element_type=jnp.float32
    )


def split(values):
    high = values.astype(jnp.bfloat16)
    return high, (values - high.astype(jnp.float32)).astype(jnp.bfloat16)


def fused_kernel(
    n_stn, n_chan, v_hbm, taps_hbm, first_hbm, twist_hbm, last_hbm, mask_hbm, out_ref,
    v_ref, taps_ref, first_ref, twist_ref, last_ref, mask_ref, in_sem, weighted, held, spec, got, pair, mine,
    own_sem, send_sem, recv_sem, back_own, back_send, back_recv,
):
    grp = lax.axis_index("grp")
    stn = lax.axis_index("stn")
    chan = lax.axis_index("chan")
    reach = out_ref.shape[0]
    chunks, _, steps, _, width = got.shape
    outer = v_ref.shape[2] // LANES
    kept = spec.shape[1]
    tap_count = taps_ref.shape[0]
    count = v_ref.shape[0] - tap_count + 1
    per_chunk = count // chunks
    sub_groups = mask_ref.shape[0]
    block = TILE // 2 * n_chan
    across = LANES // block
    me = stn * n_chan + chan
    turns = [(a, b) for a in range(n_stn) for b in range(n_chan) if (a, b) != (0, 0)]

    def partner(turn):
        return lax.rem(stn + turn[0], n_stn), lax.rem(chan + turn[1], n_chan)

    def first_row(s, c):
        return (c * n_stn + s) * steps

    ahead = per_chunk + tap_count - 1
    loads = [
        pltpu.make_async_copy(v_hbm.at[pl.ds(0, ahead)], v_ref.at[pl.ds(0, ahead)], in_sem.at[0]),
        pltpu.make_async_copy(taps_hbm, taps_ref, in_sem.at[1]),
        pltpu.make_async_copy(first_hbm, first_ref, in_sem.at[2]),
        pltpu.make_async_copy(twist_hbm, twist_ref, in_sem.at[3]),
        pltpu.make_async_copy(last_hbm, last_ref, in_sem.at[4]),
    ]
    rest = pl.ds(ahead, v_ref.shape[0] - ahead)
    later = pltpu.make_async_copy(v_hbm.at[rest], v_ref.at[rest], in_sem.at[5])
    last_load = pltpu.make_async_copy(mask_hbm, mask_ref, in_sem.at[6])
    for copy in [*loads, later, last_load]:
        copy.start()

    barrier = pltpu.get_barrier_semaphore()
    for turn in turns:
        s, c = partner(turn)
        pl.semaphore_signal(
            barrier, inc=1, device_id=(grp, s, c), device_id_type=pl.DeviceIdType.MESH
        )
    pl.semaphore_wait(barrier, len(turns))

    def own_copy(chunk):
        return pltpu.make_async_copy(
            spec.at[chunk, pl.ds(first_row(stn, chan), steps)], got.at[chunk, me], own_sem.at[chunk]
        )

    def outgoing(n, chunk):
        s, c = partner(turns[n])
        return pltpu.make_async_remote_copy(
            src_ref=spec.at[chunk, pl.ds(first_row(s, c), steps)],
            dst_ref=got.at[chunk, me],
            send_sem=send_sem.at[n, chunk],
            recv_sem=recv_sem.at[n, chunk],
            device_id=(grp, s, c),
            device_id_type=pl.DeviceIdType.MESH,
        )

    groups_here = steps * sub_groups

    def places(step):
        return pl.ds(step * sub_groups, sub_groups), pl.ds(
            stn * groups_here + step * sub_groups, sub_groups
        )

    def back_own_copy(step):
        src, dst = places(step)
        return pltpu.make_async_copy(mine.at[stn, :, src], out_ref.at[:, dst], back_own.at[step])

    def going_back(n, step):
        src, dst = places(step)
        s = lax.rem(stn + n, n_stn)
        return pltpu.make_async_remote_copy(
            src_ref=mine.at[s, :, src],
            dst_ref=out_ref.at[:, dst],
            send_sem=back_send.at[n - 1, step],
            recv_sem=back_recv.at[n - 1, step],
            device_id=(grp, s, chan),
            device_id_type=pl.DeviceIdType.MESH,
        )

    order = sorted(range(len(turns)), key=lambda n: turns[n][0] == 0)

    def one_chunk(chunk, carry):
        @pl.when(chunk == 1)
        def _():
            later.wait()

        def filter_tile(tile, inner):
            lanes = pl.ds(pl.multiple_of(tile * LANES, LANES), LANES)
            frames = [
                v_ref[chunk * per_chunk + t, :, lanes].astype(jnp.float32)
                for t in range(per_chunk + tap_count - 1)
            ]
            totals = [None] * per_chunk
            for t in range(tap_count):
                tap = jnp.broadcast_to(taps_ref[t : t + 1, lanes], (SUB, LANES))
                for s in range(per_chunk):
                    term = tap * frames[s + t]
                    totals[s] = term if t == 0 else totals[s] + term
            for s in range(per_chunk):
                weighted[pl.ds(s * SUB * outer + tile, SUB, stride=outer), :] = totals[s]
            return inner

        lax.fori_loop(0, outer, filter_tile, 0, unroll=2)

        def one_input(i, inner):
            parts = []
            for s in range(0, per_chunk, 2):
                samples = jnp.concatenate(
                    [
                        weighted[pl.ds(pl.multiple_of(((s + k) * SUB + i) * outer, outer), outer), :]
                        for k in range(2)
                    ],
                    axis=1,
                )
                high, low = split(samples)
                y = jnp.dot(
                    first_ref[...],
                    jnp.concatenate([high, high, low], axis=0),
                    preferred_element_type=jnp.float32,
                )
                for k in range(2):
                    real = y[:outer, k * LANES : (k + 1) * LANES]
                    imag = y[outer:, k * LANES : (k + 1) * LANES]
                    parts.append(
                        jnp.concatenate(
                            [
                                real * twist_ref[0] + imag * twist_ref[1],
                                imag * twist_ref[0] - real * twist_ref[1],
                            ],
                            axis=1,
                        )
                    )
            high, low = split(jnp.concatenate(parts, axis=0))
            result = (
                rows_by_rows(last_ref[0], high)
                + rows_by_rows(last_ref[1], high)
                + rows_by_rows(last_ref[0], low)
            )
            for part in range(2):
                for k in range(width // LANES):
                    held[k, pl.ds(part * SUB + i, kept, stride=TILE), :] = result[
                        part * kept : (part + 1) * kept, k * LANES : (k + 1) * LANES
                    ]
            return inner

        lax.fori_loop(0, SUB, one_input, 0, unroll=2)
        for k in range(width // LANES):
            spec[chunk, :, :, k * LANES : (k + 1) * LANES] = (
                held[k].reshape(kept, TILE, LANES).astype(jnp.bfloat16)
            )
        own_copy(chunk).start()
        for n in order:
            outgoing(n, chunk).start()
        return carry

    for copy in loads:
        copy.wait()
    lax.fori_loop(0, chunks, one_chunk, 0)
    last_load.wait()

    for chunk in range(chunks):
        own_copy(chunk).wait()
        for n in range(len(turns)):
            outgoing(n, chunk).wait_recv()

    scale = 1.0 / (count * AVG)
    n_rows = n_stn * n_chan * SUB
    lane_part = lax.broadcasted_iota(jnp.int32, (SUB, LANES), 1) // block

    def one_step(step, carry):
        columns = []
        for chunk in range(chunks):
            both = got[chunk, :, step].astype(jnp.float32)
            columns.append(
                jnp.concatenate(
                    [both[:, :SUB, :].reshape(n_rows, width), both[:, SUB:, :].reshape(n_rows, width)],
                    axis=0,
                ).astype(jnp.bfloat16)
            )
        rows = jnp.concatenate(columns, axis=1)
        total = chunks * width
        for g in range(sub_groups):
            chosen = rows.reshape(2 * n_rows // TILE, TILE, total) * mask_ref[g][None]
            product = rows_by_rows(chosen.reshape(2 * n_rows, total), rows)
            pair[g, 0] = (product[:n_rows, :n_rows] + product[n_rows:, n_rows:]) * scale
            pair[g, 1] = (product[n_rows:, :n_rows] - product[:n_rows, n_rows:]) * scale
            for b in range(n_stn):
                slabs = [
                    [pair[g, part, pl.ds(b * block + e, SUB, stride=across), :] for e in range(across)]
                    for part in range(2)
                ]
                for d in range(reach):
                    other = (b + d) % n_stn
                    tiles = []
                    for part in range(2):
                        flat = None
                        for e in range(across):
                            shift = (e - other) % across * block
                            moved = pltpu.roll(slabs[part][e], shift, 1) if shift else slabs[part][e]
                            flat = moved if flat is None else jnp.where(lane_part == e, moved, flat)
                        tiles.append(flat)
                    mine[b, d, step * sub_groups + g] = jnp.concatenate(tiles, axis=0).astype(
                        jnp.bfloat16
                    )
        back_own_copy(step).start()
        for n in range(1, n_stn):
            going_back(n, step).start()
        return carry

    lax.fori_loop(0, steps, one_step, 0)

    for chunk in range(chunks):
        for n in range(len(turns)):
            outgoing(n, chunk).wait_send()
    for step in range(steps):
        back_own_copy(step).wait()
        for n in range(1, n_stn):
            going_back(n, step).wait()


def fused(voltages, taps, n_stn, n_chan):
    inputs_here, frame_count, frame_len = voltages.shape
    count = frame_count - taps.shape[0] + 1
    outer = frame_len // LANES
    kept = frame_len // 2 // outer
    per_chunk = 2 * LANES // outer
    chunks = count // per_chunk
    width = per_chunk * outer
    peers = n_stn * n_chan - 1
    steps = kept // (n_stn * n_chan)
    sub_groups = outer // AVG
    reach = n_stn // 2 + 1
    groups = kept // n_chan * sub_groups
    mask = (np.arange(count * outer) % outer // AVG)[None, :] == np.arange(sub_groups)[:, None]
    mask = np.broadcast_to(mask[:, None, :], (sub_groups, TILE, count * outer)).astype(jnp.bfloat16)
    tables = [jnp.asarray(t) for t in (*fourier_tables(frame_len), mask)]
    frames_first = jnp.transpose(voltages, (1, 0, 2))
    vmem = pl.BlockSpec(memory_space=pltpu.VMEM)
    return pl.pallas_call(
        functools.partial(fused_kernel, n_stn, n_chan),
        in_specs=[pl.BlockSpec(memory_space=pltpu.HBM)] * (2 + len(tables)),
        out_specs=vmem,
        out_shape=jax.ShapeDtypeStruct((reach, groups, TILE, LANES), jnp.bfloat16),
        scratch_shapes=[pltpu.VMEM(a.shape, a.dtype) for a in (frames_first, taps, *tables)]
        + [
            pltpu.SemaphoreType.DMA((7,)),
            pltpu.VMEM((per_chunk * inputs_here * outer, LANES), jnp.float32),
            pltpu.VMEM((width // LANES, kept * TILE, LANES), jnp.float32),
            pltpu.VMEM((chunks, kept, TILE, width), jnp.bfloat16),
            pltpu.VMEM((chunks, n_stn * n_chan, steps, TILE, width), jnp.bfloat16),
            pltpu.VMEM((sub_groups, 2, LANES, LANES), jnp.float32),
            pltpu.VMEM((n_stn, reach, steps * sub_groups, TILE, LANES), jnp.bfloat16),
            pltpu.SemaphoreType.DMA((chunks,)),
            pltpu.SemaphoreType.DMA((peers, chunks)),
            pltpu.SemaphoreType.DMA((peers, chunks)),
            pltpu.SemaphoreType.DMA((steps,)),
            pltpu.SemaphoreType.DMA((n_stn - 1, steps)),
            pltpu.SemaphoreType.DMA((n_stn - 1, steps)),
        ],
        compiler_params=pltpu.CompilerParams(
            collective_id=0, has_side_effects=True, vmem_limit_bytes=63 * 2**20
        ),
    )(frames_first, taps, *tables)


def local(voltages, taps):
    inputs_here, frame_count, frame_len = voltages.shape
    count = frame_count - taps.shape[0] + 1
    n_stn, n_chan = lax.axis_size("stn"), lax.axis_size("chan")
    outer = frame_len // LANES
    fits = (
        inputs_here == SUB
        and inputs_here * n_stn * n_chan == LANES
        and frame_len % (LANES * AVG) == 0
        and LANES % outer == 0
        and count % (2 * LANES // outer) == 0
        and count % TILE == 0
        and count > 2 * LANES // outer
        and frame_len // 2 // outer % (n_stn * n_chan) == 0
        and (inputs_here * n_chan) ** 2 == SUB * LANES
    )
    if not fits:
        return general(voltages, taps)
    tiles = fused(voltages, taps, n_stn, n_chan)
    reach, groups = tiles.shape[:2]
    return tiles.reshape(1, reach, groups, 2, (inputs_here * n_chan) ** 2)


def solution(mesh):
    placed = (P(("grp", "stn", "chan"), None, None), P())
    return jax.shard_map(
        local,
        mesh=mesh,
        in_specs=placed,
        out_specs=P(("grp", "stn"), None, "chan", None, None),
        check_vma=False,
    )
```

```python
import functools
import math

import jax
import jax.numpy as jnp
import numpy as np
from jax import lax
from jax.experimental import pallas as pl
from jax.experimental.pallas import tpu as pltpu
from jax.sharding import PartitionSpec as P

AVG = 16


def from_behind(shard, axis, by):
    size = lax.axis_size(axis)
    return lax.ppermute(shard, axis, [(i, (i + by) % size) for i in range(size)])


def angle_table(rows, cols, modulus):
    product = (
        jnp.arange(rows, dtype=jnp.int32)[:, None]
        * jnp.arange(cols, dtype=jnp.int32)[None, :]
        % modulus
    )
    return 2.0 * math.pi / modulus * product.astype(jnp.float32)


def transform(weighted):
    rows_total = weighted.shape[0] * weighted.shape[1]
    frame_len = weighted.shape[2]
    inner = 128
    outer = frame_len // inner
    kept = frame_len // 2 // inner
    highest = lax.Precision.HIGHEST
    samples = weighted.reshape(rows_total, inner, outer)
    first = angle_table(inner, inner, inner)
    first_real = jnp.einsum("rqp,qk->rpk", samples, jnp.cos(first), precision=highest)
    first_imag = -jnp.einsum("rqp,qk->rpk", samples, jnp.sin(first), precision=highest)
    twist = angle_table(outer, inner, frame_len)
    twist_cos = jnp.cos(twist)
    twist_sin = jnp.sin(twist)
    second_real = first_real * twist_cos + first_imag * twist_sin
    second_imag = first_imag * twist_cos - first_real * twist_sin
    third = angle_table(outer, kept, outer)
    third_cos = jnp.cos(third)
    third_sin = jnp.sin(third)
    out_real = jnp.einsum("rpk,pm->rmk", second_real, third_cos, precision=highest) + jnp.einsum(
        "rpk,pm->rmk", second_imag, third_sin, precision=highest
    )
    out_imag = jnp.einsum("rpk,pm->rmk", second_imag, third_cos, precision=highest) - jnp.einsum(
        "rpk,pm->rmk", second_real, third_sin, precision=highest
    )
    scale = frame_len ** (-0.5)
    return (
        out_real.reshape(rows_total, kept * inner) * scale,
        out_imag.reshape(rows_total, kept * inner) * scale,
    )


def general(voltages, taps):
    inputs_here, frames, frame_len = voltages.shape
    tap_count = taps.shape[0]
    spectra_count = frames - tap_count + 1
    channels = frame_len // 2
    weighted = taps[0] * voltages[:, 0:spectra_count, :].astype(jnp.float32)
    for tap_index in range(1, tap_count):
        weighted = weighted + taps[tap_index] * voltages[
            :, tap_index : tap_index + spectra_count, :
        ].astype(jnp.float32)
    out_real, out_imag = transform(weighted)
    spectra = (
        jnp.stack([out_real, out_imag])
        .reshape(2, inputs_here, spectra_count, channels)
        .astype(jnp.bfloat16)
    )
    turned = lax.all_to_all(spectra, "chan", split_axis=3, concat_axis=1, tiled=True)
    block_inputs = turned.shape[1]
    chan_here = turned.shape[3]
    groups = chan_here // AVG
    scale = 1.0 / (spectra_count * AVG)
    half = lax.axis_size("stn") // 2
    reach = half + 1
    block = turned.reshape(2, block_inputs, spectra_count, groups, AVG)
    block = block.transpose(3, 0, 1, 2, 4).reshape(groups, 2 * block_inputs, spectra_count * AVG)

    def correlate(own, other):
        product = jnp.einsum("gak,gck->gac", own, other, preferred_element_type=jnp.float32)
        real_vis = (
            product[:, :block_inputs, :block_inputs] + product[:, block_inputs:, block_inputs:]
        )
        imag_vis = (
            product[:, block_inputs:, :block_inputs] - product[:, :block_inputs, block_inputs:]
        )
        both = jnp.stack([real_vis, imag_vis], axis=1).reshape(
            groups, 2, block_inputs * block_inputs
        )
        return (both * scale).astype(jnp.bfloat16)

    tiles = jnp.zeros((reach, groups, 2, block_inputs * block_inputs), jnp.bfloat16)
    tiles = tiles.at[0].set(correlate(block, block))

    def advance(distance, carry):
        moving, stack_now = carry
        moving = from_behind(moving, "stn", -1)
        stack_now = lax.dynamic_update_index_in_dim(
            stack_now, correlate(block, moving), distance, 0
        )
        return (moving, stack_now)

    moved, tiles = lax.fori_loop(1, reach, advance, (block, tiles))
    return tiles[None]


LANES = 128
SUB = 8
TILE = 16


def halves(table):
    high = table.astype(jnp.bfloat16)
    low = (table - high.astype(np.float64)).astype(jnp.bfloat16)
    return high, low


def fourier_tables(frame_len):
    outer = frame_len // LANES
    kept = frame_len // 2 // outer
    high_digit = np.arange(outer)
    lane = np.arange(LANES)
    first = 2.0 * np.pi / outer * (np.outer(high_digit, high_digit) % outer)
    first = np.concatenate([np.cos(first), -np.sin(first)], axis=0)
    high, low = halves(first)
    first = np.concatenate([high, low, high], axis=1)
    twist = 2.0 * np.pi / frame_len * (np.outer(high_digit, lane) % frame_len)
    last = 2.0 * np.pi / LANES * (np.outer(np.arange(kept), lane) % LANES)
    cos, sin = np.cos(last), np.sin(last)
    last = np.concatenate(
        [np.concatenate([cos, sin], axis=1), np.concatenate([-sin, cos], axis=1)], axis=0
    )
    high, low = halves(last * frame_len ** (-0.5))
    last = np.stack([high, low])
    return first, np.stack([np.cos(twist), np.sin(twist)]).astype(np.float32), last


def rows_by_rows(left, right):
    return lax.dot_general(
        left, right, (((1,), (1,)), ((), ())), preferred_element_type=jnp.float32
    )


def split(values):
    high = values.astype(jnp.bfloat16)
    return high, (values - high.astype(jnp.float32)).astype(jnp.bfloat16)


def fused_kernel(
    n_stn, n_chan, v_hbm, taps_hbm, first_hbm, twist_hbm, last_hbm, mask_hbm, out_ref,
    v_ref, taps_ref, first_ref, twist_ref, last_ref, mask_ref, in_sem, weighted, held, spec, got, pair, mine,
    own_sem, send_sem, recv_sem, back_own, back_send, back_recv,
    near, near_pair, near_mine, near_own, near_send, near_recv,
    near_back_own, near_back_send, near_back_recv,
):
    grp = lax.axis_index("grp")
    stn = lax.axis_index("stn")
    chan = lax.axis_index("chan")
    reach = out_ref.shape[0]
    chunks, _, steps, _, width = got.shape
    outer = v_ref.shape[2] // LANES
    kept = spec.shape[1]
    tap_count = taps_ref.shape[0]
    count = v_ref.shape[0] - tap_count + 1
    per_chunk = count // chunks
    sub_groups = mask_ref.shape[0]
    block = TILE // 2 * n_chan
    across = LANES // block
    me = stn * n_chan + chan
    turns = [(a, b) for a in range(n_stn) for b in range(n_chan) if (a, b) != (0, 0)]

    half = n_stn // 2
    within = lax.rem(stn, half)
    base = stn - within
    me_near = within * n_chan + chan
    near_turns = [(a, b) for a in range(half) for b in range(n_chan) if (a, b) != (0, 0)]

    def twin(s):
        return lax.rem(s + half, n_stn)

    def neighbour(a):
        return base + lax.rem(within + a, half)

    def partner(turn):
        return lax.rem(stn + turn[0], n_stn), lax.rem(chan + turn[1], n_chan)

    def first_row(s, c):
        return (c * n_stn + s) * steps

    ahead = per_chunk + tap_count - 1
    loads = [
        pltpu.make_async_copy(v_hbm.at[pl.ds(0, ahead)], v_ref.at[pl.ds(0, ahead)], in_sem.at[0]),
        pltpu.make_async_copy(taps_hbm, taps_ref, in_sem.at[1]),
        pltpu.make_async_copy(first_hbm, first_ref, in_sem.at[2]),
        pltpu.make_async_copy(twist_hbm, twist_ref, in_sem.at[3]),
        pltpu.make_async_copy(last_hbm, last_ref, in_sem.at[4]),
    ]
    rest = pl.ds(ahead, v_ref.shape[0] - ahead)
    later = pltpu.make_async_copy(v_hbm.at[rest], v_ref.at[rest], in_sem.at[5])
    last_load = pltpu.make_async_copy(mask_hbm, mask_ref, in_sem.at[6])
    for copy in [*loads, later, last_load]:
        copy.start()

    barrier = pltpu.get_barrier_semaphore()
    for turn in turns:
        s, c = partner(turn)
        pl.semaphore_signal(
            barrier, inc=1, device_id=(grp, s, c), device_id_type=pl.DeviceIdType.MESH
        )
    pl.semaphore_wait(barrier, len(turns))

    def own_copy(chunk):
        return pltpu.make_async_copy(
            spec.at[chunk, pl.ds(first_row(stn, chan), steps)], got.at[chunk, me], own_sem.at[chunk]
        )

    def outgoing(n, chunk):
        s, c = partner(turns[n])
        return pltpu.make_async_remote_copy(
            src_ref=spec.at[chunk, pl.ds(first_row(s, c), steps)],
            dst_ref=got.at[chunk, me],
            send_sem=send_sem.at[n, chunk],
            recv_sem=recv_sem.at[n, chunk],
            device_id=(grp, s, c),
            device_id_type=pl.DeviceIdType.MESH,
        )

    def near_own_copy(chunk):
        return pltpu.make_async_copy(
            spec.at[chunk, pl.ds(first_row(twin(stn), chan), steps)],
            near.at[chunk, me_near],
            near_own.at[chunk],
        )

    def near_outgoing(n, chunk):
        s, c = neighbour(near_turns[n][0]), lax.rem(chan + near_turns[n][1], n_chan)
        return pltpu.make_async_remote_copy(
            src_ref=spec.at[chunk, pl.ds(first_row(twin(s), c), steps)],
            dst_ref=near.at[chunk, me_near],
            send_sem=near_send.at[n, chunk],
            recv_sem=near_recv.at[n, chunk],
            device_id=(grp, s, c),
            device_id_type=pl.DeviceIdType.MESH,
        )

    groups_here = steps * sub_groups

    def places(step, part):
        return pl.ds(step * sub_groups, sub_groups), pl.ds(
            part * groups_here + step * sub_groups, sub_groups
        )

    def back_own_copy(step):
        src, dst = places(step, stn)
        return pltpu.make_async_copy(mine.at[stn, :, src], out_ref.at[:, dst], back_own.at[step])

    def going_back(n, d, step):
        src, dst = places(step, stn)
        s = lax.rem(stn + n, n_stn)
        return pltpu.make_async_remote_copy(
            src_ref=mine.at[s, d, src],
            dst_ref=out_ref.at[d, dst],
            send_sem=back_send.at[n - 1, d, step],
            recv_sem=back_recv.at[n - 1, d, step],
            device_id=(grp, s, chan),
            device_id_type=pl.DeviceIdType.MESH,
        )

    def near_back_own_copy(d, step):
        src, dst = places(step, twin(stn))
        return pltpu.make_async_copy(
            near_mine.at[within, d, src], out_ref.at[d, dst], near_back_own.at[d, step]
        )

    def near_going_back(a, d, step):
        src, dst = places(step, twin(stn))
        s = neighbour(a)
        return pltpu.make_async_remote_copy(
            src_ref=near_mine.at[lax.rem(within + a, half), d, src],
            dst_ref=out_ref.at[d, dst],
            send_sem=near_back_send.at[a - 1, d, step],
            recv_sem=near_back_recv.at[a - 1, d, step],
            device_id=(grp, s, chan),
            device_id_type=pl.DeviceIdType.MESH,
        )

    def owed(worker, owner, d):
        place = lax.rem(owner, half)
        same = worker - lax.rem(worker, half) == owner - place
        return jnp.logical_or(same, place + d >= half)

    def stays(owner, d):
        return lax.rem(owner, half) + d < half

    def each_back(act):
        for n in range(1, n_stn):
            for d in range(reach):
                act(n, d)

    order = sorted(range(len(turns)), key=lambda n: turns[n][0] == 0)

    def one_chunk(chunk, carry):
        @pl.when(chunk == 1)
        def _():
            later.wait()

        def filter_tile(tile, inner):
            lanes = pl.ds(pl.multiple_of(tile * LANES, LANES), LANES)
            frames = [
                v_ref[chunk * per_chunk + t, :, lanes].astype(jnp.float32)
                for t in range(per_chunk + tap_count - 1)
            ]
            totals = [None] * per_chunk
            for t in range(tap_count):
                tap = jnp.broadcast_to(taps_ref[t : t + 1, lanes], (SUB, LANES))
                for s in range(per_chunk):
                    term = tap * frames[s + t]
                    totals[s] = term if t == 0 else totals[s] + term
            for s in range(per_chunk):
                weighted[pl.ds(s * SUB * outer + tile, SUB, stride=outer), :] = totals[s]
            return inner

        lax.fori_loop(0, outer, filter_tile, 0, unroll=2)

        def one_input(i, inner):
            parts = []
            for s in range(0, per_chunk, 2):
                samples = jnp.concatenate(
                    [
                        weighted[pl.ds(pl.multiple_of(((s + k) * SUB + i) * outer, outer), outer), :]
                        for k in range(2)
                    ],
                    axis=1,
                )
                high, low = split(samples)
                y = jnp.dot(
                    first_ref[...],
                    jnp.concatenate([high, high, low], axis=0),
                    preferred_element_type=jnp.float32,
                )
                for k in range(2):
                    real = y[:outer, k * LANES : (k + 1) * LANES]
                    imag = y[outer:, k * LANES : (k + 1) * LANES]
                    parts.append(
                        jnp.concatenate(
                            [
                                real * twist_ref[0] + imag * twist_ref[1],
                                imag * twist_ref[0] - real * twist_ref[1],
                            ],
                            axis=1,
                        )
                    )
            high, low = split(jnp.concatenate(parts, axis=0))
            result = (
                rows_by_rows(last_ref[0], high)
                + rows_by_rows(last_ref[1], high)
                + rows_by_rows(last_ref[0], low)
            )
            for part in range(2):
                for k in range(width // LANES):
                    held[k, pl.ds(part * SUB + i, kept, stride=TILE), :] = result[
                        part * kept : (part + 1) * kept, k * LANES : (k + 1) * LANES
                    ]
            return inner

        lax.fori_loop(0, SUB, one_input, 0, unroll=2)
        for k in range(width // LANES):
            spec[chunk, :, :, k * LANES : (k + 1) * LANES] = (
                held[k].reshape(kept, TILE, LANES).astype(jnp.bfloat16)
            )
        own_copy(chunk).start()
        for n in order:
            outgoing(n, chunk).start()
        near_own_copy(chunk).start()
        for n in range(len(near_turns)):
            near_outgoing(n, chunk).start()
        return carry

    for copy in loads:
        copy.wait()
    lax.fori_loop(0, chunks, one_chunk, 0)
    last_load.wait()

    for chunk in range(chunks):
        own_copy(chunk).wait()
        for n in range(len(turns)):
            outgoing(n, chunk).wait_recv()

    scale = 1.0 / (count * AVG)
    n_rows = n_stn * n_chan * SUB
    lane_part = lax.broadcasted_iota(jnp.int32, (SUB, LANES), 1) // block

    def stack(buffer, step):
        columns = []
        for chunk in range(chunks):
            both = buffer[chunk, :, step].astype(jnp.float32)
            rows = both.shape[0] * SUB
            columns.append(
                jnp.concatenate(
                    [both[:, :SUB, :].reshape(rows, width), both[:, SUB:, :].reshape(rows, width)],
                    axis=0,
                ).astype(jnp.bfloat16)
            )
        return jnp.concatenate(columns, axis=1)

    def products(rows, g):
        total = chunks * width
        chosen = rows.reshape(rows.shape[0] // TILE, TILE, total) * mask_ref[g][None]
        return rows_by_rows(chosen.reshape(rows.shape[0], total), rows)

    def slabs_of(source, g, b):
        return [
            [source[g, part, pl.ds(b * block + e, SUB, stride=across), :] for e in range(across)]
            for part in range(2)
        ]

    def flatten(slabs, other):
        tiles = []
        for part in range(2):
            flat = None
            for e in range(across):
                shift = (e - other) % across * block
                moved = pltpu.roll(slabs[part][e], shift, 1) if shift else slabs[part][e]
                flat = moved if flat is None else jnp.where(lane_part == e, moved, flat)
            tiles.append(flat)
        return jnp.concatenate(tiles, axis=0).astype(jnp.bfloat16)

    def one_step(step, carry):
        rows = stack(got, step)
        for g in range(sub_groups):
            product = products(rows, g)
            pair[g, 0] = (product[:n_rows, :n_rows] + product[n_rows:, n_rows:]) * scale
            pair[g, 1] = (product[n_rows:, :n_rows] - product[:n_rows, n_rows:]) * scale
            for b in range(n_stn):
                slabs = slabs_of(pair, g, b)
                for d in range(reach):
                    mine[b, d, step * sub_groups + g] = flatten(slabs, (b + d) % n_stn)
        back_own_copy(step).start()

        def send(n, d):
            @pl.when(owed(stn, lax.rem(stn + n, n_stn), d))
            def _():
                going_back(n, d, step).start()

        each_back(send)
        return carry

    lax.fori_loop(0, steps, one_step, 0)

    for chunk in range(chunks):
        near_own_copy(chunk).wait()
        for n in range(len(near_turns)):
            near_outgoing(n, chunk).wait_recv()

    near_rows = half * n_chan * SUB

    def near_step(step, carry):
        rows = stack(near, step)
        for g in range(sub_groups):
            product = products(rows, g)
            turned = pltpu.roll(product, near_rows, 1)
            near_pair[g, 0] = (product[:near_rows] + turned[near_rows:]) * scale
            near_pair[g, 1] = (product[near_rows:] - turned[:near_rows]) * scale
            for b in range(half):
                slabs = slabs_of(near_pair, g, b)
                for d in range(half - b):
                    near_mine[b, d, step * sub_groups + g] = flatten(slabs, b + d)
        for d in range(half):

            @pl.when(stays(stn, d))
            def _():
                near_back_own_copy(d, step).start()

            for a in range(1, half):

                @pl.when(stays(neighbour(a), d))
                def _():
                    near_going_back(a, d, step).start()

        return carry

    lax.fori_loop(0, steps, near_step, 0)

    for chunk in range(chunks):
        for n in range(len(turns)):
            outgoing(n, chunk).wait_send()
        for n in range(len(near_turns)):
            near_outgoing(n, chunk).wait_send()

    def finish(step, carry):
        back_own_copy(step).wait()

        def end(n, d):
            @pl.when(owed(stn, lax.rem(stn + n, n_stn), d))
            def _():
                going_back(n, d, step).wait_send()

            @pl.when(owed(lax.rem(stn - n + n_stn, n_stn), stn, d))
            def _():
                going_back(n, d, step).wait_recv()

        each_back(end)
        for d in range(half):

            @pl.when(stays(stn, d))
            def _():
                near_back_own_copy(d, step).wait()

            for a in range(1, half):

                @pl.when(stays(neighbour(a), d))
                def _():
                    near_going_back(a, d, step).wait_send()

                @pl.when(stays(stn, d))
                def _():
                    near_going_back(a, d, step).wait_recv()

        return carry

    lax.fori_loop(0, steps, finish, 0)


def fused(voltages, taps, n_stn, n_chan):
    inputs_here, frame_count, frame_len = voltages.shape
    count = frame_count - taps.shape[0] + 1
    outer = frame_len // LANES
    kept = frame_len // 2 // outer
    per_chunk = 2 * LANES // outer
    chunks = count // per_chunk
    width = per_chunk * outer
    peers = n_stn * n_chan - 1
    steps = kept // (n_stn * n_chan)
    sub_groups = outer // AVG
    half = n_stn // 2
    reach = half + 1
    groups = kept // n_chan * sub_groups
    mask = (np.arange(count * outer) % outer // AVG)[None, :] == np.arange(sub_groups)[:, None]
    mask = np.broadcast_to(mask[:, None, :], (sub_groups, TILE, count * outer)).astype(jnp.bfloat16)
    tables = [jnp.asarray(t) for t in (*fourier_tables(frame_len), mask)]
    frames_first = jnp.transpose(voltages, (1, 0, 2))
    vmem = pl.BlockSpec(memory_space=pltpu.VMEM)
    return pl.pallas_call(
        functools.partial(fused_kernel, n_stn, n_chan),
        in_specs=[pl.BlockSpec(memory_space=pltpu.HBM)] * (2 + len(tables)),
        out_specs=vmem,
        out_shape=jax.ShapeDtypeStruct((reach, groups, TILE, LANES), jnp.bfloat16),
        scratch_shapes=[pltpu.VMEM(a.shape, a.dtype) for a in (frames_first, taps, *tables)]
        + [
            pltpu.SemaphoreType.DMA((7,)),
            pltpu.VMEM((per_chunk * inputs_here * outer, LANES), jnp.float32),
            pltpu.VMEM((width // LANES, kept * TILE, LANES), jnp.float32),
            pltpu.VMEM((chunks, kept, TILE, width), jnp.bfloat16),
            pltpu.VMEM((chunks, n_stn * n_chan, steps, TILE, width), jnp.bfloat16),
            pltpu.VMEM((sub_groups, 2, LANES, LANES), jnp.float32),
            pltpu.VMEM((n_stn, reach, steps * sub_groups, TILE, LANES), jnp.bfloat16),
            pltpu.SemaphoreType.DMA((chunks,)),
            pltpu.SemaphoreType.DMA((peers, chunks)),
            pltpu.SemaphoreType.DMA((peers, chunks)),
            pltpu.SemaphoreType.DMA((steps,)),
            pltpu.SemaphoreType.DMA((n_stn - 1, reach, steps)),
            pltpu.SemaphoreType.DMA((n_stn - 1, reach, steps)),
            pltpu.VMEM((chunks, half * n_chan, steps, TILE, width), jnp.bfloat16),
            pltpu.VMEM((sub_groups, 2, half * n_chan * SUB, LANES), jnp.float32),
            pltpu.VMEM((half, half, steps * sub_groups, TILE, LANES), jnp.bfloat16),
            pltpu.SemaphoreType.DMA((chunks,)),
            pltpu.SemaphoreType.DMA((half * n_chan - 1, chunks)),
            pltpu.SemaphoreType.DMA((half * n_chan - 1, chunks)),
            pltpu.SemaphoreType.DMA((half, steps)),
            pltpu.SemaphoreType.DMA((half - 1, half, steps)),
            pltpu.SemaphoreType.DMA((half - 1, half, steps)),
        ],
        compiler_params=pltpu.CompilerParams(
            collective_id=0, has_side_effects=True, vmem_limit_bytes=63 * 2**20
        ),
    )(frames_first, taps, *tables)


def local(voltages, taps):
    inputs_here, frame_count, frame_len = voltages.shape
    count = frame_count - taps.shape[0] + 1
    n_stn, n_chan = lax.axis_size("stn"), lax.axis_size("chan")
    outer = frame_len // LANES
    fits = (
        inputs_here == SUB
        and inputs_here * n_stn * n_chan == LANES
        and frame_len % (LANES * AVG) == 0
        and LANES % outer == 0
        and count % (2 * LANES // outer) == 0
        and count % TILE == 0
        and n_stn % 2 == 0
        and n_stn > 2
        and count > 2 * LANES // outer
        and frame_len // 2 // outer % (n_stn * n_chan) == 0
        and (inputs_here * n_chan) ** 2 == SUB * LANES
    )
    if not fits:
        return general(voltages, taps)
    tiles = fused(voltages, taps, n_stn, n_chan)
    reach, groups = tiles.shape[:2]
    return tiles.reshape(1, reach, groups, 2, (inputs_here * n_chan) ** 2)


def solution(mesh):
    placed = (P(("grp", "stn", "chan"), None, None), P())
    return jax.shard_map(
        local,
        mesh=mesh,
        in_specs=placed,
        out_specs=P(("grp", "stn"), None, "chan", None, None),
        check_vma=False,
    )
```

```python
import functools
import math

import jax
import jax.numpy as jnp
import numpy as np
from jax import lax
from jax.experimental import pallas as pl
from jax.experimental.pallas import tpu as pltpu
from jax.sharding import PartitionSpec as P

AVG = 16


def from_behind(shard, axis, by):
    size = lax.axis_size(axis)
    return lax.ppermute(shard, axis, [(i, (i + by) % size) for i in range(size)])


def angle_table(rows, cols, modulus):
    product = (
        jnp.arange(rows, dtype=jnp.int32)[:, None]
        * jnp.arange(cols, dtype=jnp.int32)[None, :]
        % modulus
    )
    return 2.0 * math.pi / modulus * product.astype(jnp.float32)


def transform(weighted):
    rows_total = weighted.shape[0] * weighted.shape[1]
    frame_len = weighted.shape[2]
    inner = 128
    outer = frame_len // inner
    kept = frame_len // 2 // inner
    highest = lax.Precision.HIGHEST
    samples = weighted.reshape(rows_total, inner, outer)
    first = angle_table(inner, inner, inner)
    first_real = jnp.einsum("rqp,qk->rpk", samples, jnp.cos(first), precision=highest)
    first_imag = -jnp.einsum("rqp,qk->rpk", samples, jnp.sin(first), precision=highest)
    twist = angle_table(outer, inner, frame_len)
    twist_cos = jnp.cos(twist)
    twist_sin = jnp.sin(twist)
    second_real = first_real * twist_cos + first_imag * twist_sin
    second_imag = first_imag * twist_cos - first_real * twist_sin
    third = angle_table(outer, kept, outer)
    third_cos = jnp.cos(third)
    third_sin = jnp.sin(third)
    out_real = jnp.einsum("rpk,pm->rmk", second_real, third_cos, precision=highest) + jnp.einsum(
        "rpk,pm->rmk", second_imag, third_sin, precision=highest
    )
    out_imag = jnp.einsum("rpk,pm->rmk", second_imag, third_cos, precision=highest) - jnp.einsum(
        "rpk,pm->rmk", second_real, third_sin, precision=highest
    )
    scale = frame_len ** (-0.5)
    return (
        out_real.reshape(rows_total, kept * inner) * scale,
        out_imag.reshape(rows_total, kept * inner) * scale,
    )


def general(voltages, taps):
    inputs_here, frames, frame_len = voltages.shape
    tap_count = taps.shape[0]
    spectra_count = frames - tap_count + 1
    channels = frame_len // 2
    weighted = taps[0] * voltages[:, 0:spectra_count, :].astype(jnp.float32)
    for tap_index in range(1, tap_count):
        weighted = weighted + taps[tap_index] * voltages[
            :, tap_index : tap_index + spectra_count, :
        ].astype(jnp.float32)
    out_real, out_imag = transform(weighted)
    spectra = (
        jnp.stack([out_real, out_imag])
        .reshape(2, inputs_here, spectra_count, channels)
        .astype(jnp.bfloat16)
    )
    turned = lax.all_to_all(spectra, "chan", split_axis=3, concat_axis=1, tiled=True)
    block_inputs = turned.shape[1]
    chan_here = turned.shape[3]
    groups = chan_here // AVG
    scale = 1.0 / (spectra_count * AVG)
    half = lax.axis_size("stn") // 2
    reach = half + 1
    block = turned.reshape(2, block_inputs, spectra_count, groups, AVG)
    block = block.transpose(3, 0, 1, 2, 4).reshape(groups, 2 * block_inputs, spectra_count * AVG)

    def correlate(own, other):
        product = jnp.einsum("gak,gck->gac", own, other, preferred_element_type=jnp.float32)
        real_vis = (
            product[:, :block_inputs, :block_inputs] + product[:, block_inputs:, block_inputs:]
        )
        imag_vis = (
            product[:, block_inputs:, :block_inputs] - product[:, :block_inputs, block_inputs:]
        )
        both = jnp.stack([real_vis, imag_vis], axis=1).reshape(
            groups, 2, block_inputs * block_inputs
        )
        return (both * scale).astype(jnp.bfloat16)

    tiles = jnp.zeros((reach, groups, 2, block_inputs * block_inputs), jnp.bfloat16)
    tiles = tiles.at[0].set(correlate(block, block))

    def advance(distance, carry):
        moving, stack_now = carry
        moving = from_behind(moving, "stn", -1)
        stack_now = lax.dynamic_update_index_in_dim(
            stack_now, correlate(block, moving), distance, 0
        )
        return (moving, stack_now)

    moved, tiles = lax.fori_loop(1, reach, advance, (block, tiles))
    return tiles[None]


LANES = 128
SUB = 8
TILE = 16


def halves(table):
    high = table.astype(jnp.bfloat16)
    low = (table - high.astype(np.float64)).astype(jnp.bfloat16)
    return high, low


def fourier_tables(frame_len):
    outer = frame_len // LANES
    kept = frame_len // 2 // outer
    high_digit = np.arange(outer)
    lane = np.arange(LANES)
    first = 2.0 * np.pi / outer * (np.outer(high_digit, high_digit) % outer)
    first = np.concatenate([np.cos(first), -np.sin(first)], axis=0)
    high, low = halves(first)
    first = np.concatenate([high, low, high], axis=1)
    twist = 2.0 * np.pi / frame_len * (np.outer(high_digit, lane) % frame_len)
    last = 2.0 * np.pi / LANES * (np.outer(np.arange(kept), lane) % LANES)
    cos, sin = np.cos(last), np.sin(last)
    last = np.concatenate(
        [np.concatenate([cos, sin], axis=1), np.concatenate([-sin, cos], axis=1)], axis=0
    )
    high, low = halves(last * frame_len ** (-0.5))
    last = np.stack([high, low])
    return first, np.stack([np.cos(twist), np.sin(twist)]).astype(np.float32), last


def rows_by_rows(left, right):
    return lax.dot_general(
        left, right, (((1,), (1,)), ((), ())), preferred_element_type=jnp.float32
    )


def split(values):
    high = values.astype(jnp.bfloat16)
    return high, (values - high.astype(jnp.float32)).astype(jnp.bfloat16)


def fused_kernel(
    n_stn, n_chan, v_hbm, taps_hbm, first_hbm, twist_hbm, last_hbm, mask_hbm, out_ref,
    v_ref, taps_ref, first_ref, twist_ref, last_ref, mask_ref, in_sem, weighted, held, spec, got, pair, mine,
    own_sem, send_sem, recv_sem, back_own, back_send, back_recv,
    near, near_pair, near_mine, near_own, near_send, near_recv,
    near_back_own, near_back_send, near_back_recv,
):
    grp = lax.axis_index("grp")
    stn = lax.axis_index("stn")
    chan = lax.axis_index("chan")
    reach = out_ref.shape[0]
    chunks, _, steps, _, width = got.shape
    outer = v_ref.shape[2] // LANES
    kept = spec.shape[1]
    tap_count = taps_ref.shape[0]
    count = v_ref.shape[0] - tap_count + 1
    per_chunk = count // chunks
    sub_groups = mask_ref.shape[0]
    block = TILE // 2 * n_chan
    across = LANES // block
    me = stn * n_chan + chan
    turns = [(a, b) for a in range(n_stn) for b in range(n_chan) if (a, b) != (0, 0)]

    half = n_stn // 2
    within = lax.rem(stn, half)
    base = stn - within
    me_near = within * n_chan + chan
    near_turns = [(a, b) for a in range(half) for b in range(n_chan) if (a, b) != (0, 0)]

    def twin(s):
        return lax.rem(s + half, n_stn)

    def neighbour(a):
        return base + lax.rem(within + a, half)

    def partner(turn):
        return lax.rem(stn + turn[0], n_stn), lax.rem(chan + turn[1], n_chan)

    def first_row(s, c):
        return (c * n_stn + s) * steps

    ahead = per_chunk + tap_count - 1
    loads = [
        pltpu.make_async_copy(v_hbm.at[pl.ds(0, ahead)], v_ref.at[pl.ds(0, ahead)], in_sem.at[0]),
        pltpu.make_async_copy(taps_hbm, taps_ref, in_sem.at[1]),
        pltpu.make_async_copy(first_hbm, first_ref, in_sem.at[2]),
        pltpu.make_async_copy(twist_hbm, twist_ref, in_sem.at[3]),
        pltpu.make_async_copy(last_hbm, last_ref, in_sem.at[4]),
    ]
    rest = pl.ds(ahead, v_ref.shape[0] - ahead)
    later = pltpu.make_async_copy(v_hbm.at[rest], v_ref.at[rest], in_sem.at[5])
    last_load = pltpu.make_async_copy(mask_hbm, mask_ref, in_sem.at[6])
    for copy in [*loads, later, last_load]:
        copy.start()

    barrier = pltpu.get_barrier_semaphore()
    for turn in turns:
        s, c = partner(turn)
        pl.semaphore_signal(
            barrier, inc=1, device_id=(grp, s, c), device_id_type=pl.DeviceIdType.MESH
        )
    pl.semaphore_wait(barrier, len(turns))

    def own_copy(chunk):
        return pltpu.make_async_copy(
            spec.at[chunk, pl.ds(first_row(stn, chan), steps)], got.at[chunk, me], own_sem.at[chunk]
        )

    def outgoing(n, chunk):
        s, c = partner(turns[n])
        return pltpu.make_async_remote_copy(
            src_ref=spec.at[chunk, pl.ds(first_row(s, c), steps)],
            dst_ref=got.at[chunk, me],
            send_sem=send_sem.at[n, chunk],
            recv_sem=recv_sem.at[n, chunk],
            device_id=(grp, s, c),
            device_id_type=pl.DeviceIdType.MESH,
        )

    def near_own_copy(chunk):
        return pltpu.make_async_copy(
            spec.at[chunk, pl.ds(first_row(twin(stn), chan), steps)],
            near.at[chunk, me_near],
            near_own.at[chunk],
        )

    def near_outgoing(n, chunk):
        s, c = neighbour(near_turns[n][0]), lax.rem(chan + near_turns[n][1], n_chan)
        return pltpu.make_async_remote_copy(
            src_ref=spec.at[chunk, pl.ds(first_row(twin(s), c), steps)],
            dst_ref=near.at[chunk, me_near],
            send_sem=near_send.at[n, chunk],
            recv_sem=near_recv.at[n, chunk],
            device_id=(grp, s, c),
            device_id_type=pl.DeviceIdType.MESH,
        )

    groups_here = steps * sub_groups

    def places(step, part):
        return pl.ds(step * sub_groups, sub_groups), pl.ds(
            part * groups_here + step * sub_groups, sub_groups
        )

    def back_own_copy(step):
        src, dst = places(step, stn)
        return pltpu.make_async_copy(mine.at[stn, :, src], out_ref.at[:, dst], back_own.at[step])

    def going_back(n, d, step):
        src, dst = places(step, stn)
        s = lax.rem(stn + n, n_stn)
        return pltpu.make_async_remote_copy(
            src_ref=mine.at[s, d, src],
            dst_ref=out_ref.at[d, dst],
            send_sem=back_send.at[n - 1, d, step],
            recv_sem=back_recv.at[n - 1, d, step],
            device_id=(grp, s, chan),
            device_id_type=pl.DeviceIdType.MESH,
        )

    def near_back_own_copy(d, step):
        src, dst = places(step, twin(stn))
        return pltpu.make_async_copy(
            near_mine.at[within, d, src], out_ref.at[d, dst], near_back_own.at[d, step]
        )

    def near_going_back(a, d, step):
        src, dst = places(step, twin(stn))
        s = neighbour(a)
        return pltpu.make_async_remote_copy(
            src_ref=near_mine.at[lax.rem(within + a, half), d, src],
            dst_ref=out_ref.at[d, dst],
            send_sem=near_back_send.at[a - 1, d, step],
            recv_sem=near_back_recv.at[a - 1, d, step],
            device_id=(grp, s, chan),
            device_id_type=pl.DeviceIdType.MESH,
        )

    def owed(worker, owner, d):
        place = lax.rem(owner, half)
        same = worker - lax.rem(worker, half) == owner - place
        return jnp.logical_or(same, place + d >= half)

    def stays(owner, d):
        return lax.rem(owner, half) + d < half

    def each_back(act):
        for n in range(1, n_stn):
            for d in range(reach):
                act(n, d)

    order = sorted(range(len(turns)), key=lambda n: turns[n][0] == 0)

    def one_chunk(chunk, carry):
        @pl.when(chunk == 1)
        def _():
            later.wait()

        def filter_tile(tile, inner):
            lanes = pl.ds(pl.multiple_of(tile * LANES, LANES), LANES)
            frames = [
                v_ref[chunk * per_chunk + t, :, lanes].astype(jnp.float32)
                for t in range(per_chunk + tap_count - 1)
            ]
            totals = [None] * per_chunk
            for t in range(tap_count):
                tap = jnp.broadcast_to(taps_ref[t : t + 1, lanes], (SUB, LANES))
                for s in range(per_chunk):
                    term = tap * frames[s + t]
                    totals[s] = term if t == 0 else totals[s] + term
            for s in range(per_chunk):
                weighted[pl.ds(s * SUB * outer + tile, SUB, stride=outer), :] = totals[s]
            return inner

        lax.fori_loop(0, outer, filter_tile, 0, unroll=2)

        def one_input(i, inner):
            parts = []
            for s in range(0, per_chunk, 2):
                samples = jnp.concatenate(
                    [
                        weighted[pl.ds(pl.multiple_of(((s + k) * SUB + i) * outer, outer), outer), :]
                        for k in range(2)
                    ],
                    axis=1,
                )
                high, low = split(samples)
                y = jnp.dot(
                    first_ref[...],
                    jnp.concatenate([high, high, low], axis=0),
                    preferred_element_type=jnp.float32,
                )
                for k in range(2):
                    real = y[:outer, k * LANES : (k + 1) * LANES]
                    imag = y[outer:, k * LANES : (k + 1) * LANES]
                    parts.append(
                        jnp.concatenate(
                            [
                                real * twist_ref[0] + imag * twist_ref[1],
                                imag * twist_ref[0] - real * twist_ref[1],
                            ],
                            axis=1,
                        )
                    )
            high, low = split(jnp.concatenate(parts, axis=0))
            result = (
                rows_by_rows(last_ref[0], high)
                + rows_by_rows(last_ref[1], high)
                + rows_by_rows(last_ref[0], low)
            )
            for part in range(2):
                for k in range(width // LANES):
                    held[k, pl.ds(part * SUB + i, kept, stride=TILE), :] = result[
                        part * kept : (part + 1) * kept, k * LANES : (k + 1) * LANES
                    ]
            return inner

        lax.fori_loop(0, SUB, one_input, 0, unroll=2)
        for k in range(width // LANES):
            spec[chunk, :, :, k * LANES : (k + 1) * LANES] = (
                held[k].reshape(kept, TILE, LANES).astype(jnp.bfloat16)
            )
        near_own_copy(chunk).start()
        for n in range(len(near_turns)):
            near_outgoing(n, chunk).start()
        own_copy(chunk).start()
        for n in order:
            outgoing(n, chunk).start()
        return carry

    for copy in loads:
        copy.wait()
    lax.fori_loop(0, chunks, one_chunk, 0)
    last_load.wait()

    scale = 1.0 / (count * AVG)
    n_rows = n_stn * n_chan * SUB
    lane_part = lax.broadcasted_iota(jnp.int32, (SUB, LANES), 1) // block

    def stack(buffer, step):
        columns = []
        for chunk in range(chunks):
            both = buffer[chunk, :, step].astype(jnp.float32)
            rows = both.shape[0] * SUB
            columns.append(
                jnp.concatenate(
                    [both[:, :SUB, :].reshape(rows, width), both[:, SUB:, :].reshape(rows, width)],
                    axis=0,
                ).astype(jnp.bfloat16)
            )
        return jnp.concatenate(columns, axis=1)

    def products(rows, g):
        total = chunks * width
        chosen = rows.reshape(rows.shape[0] // TILE, TILE, total) * mask_ref[g][None]
        return rows_by_rows(chosen.reshape(rows.shape[0], total), rows)

    def slabs_of(source, g, b):
        return [
            [source[g, part, pl.ds(b * block + e, SUB, stride=across), :] for e in range(across)]
            for part in range(2)
        ]

    def flatten(slabs, other):
        tiles = []
        for part in range(2):
            flat = None
            for e in range(across):
                shift = (e - other) % across * block
                moved = pltpu.roll(slabs[part][e], shift, 1) if shift else slabs[part][e]
                flat = moved if flat is None else jnp.where(lane_part == e, moved, flat)
            tiles.append(flat)
        return jnp.concatenate(tiles, axis=0).astype(jnp.bfloat16)

    def one_step(step, carry):
        rows = stack(got, step)
        for g in range(sub_groups):
            product = products(rows, g)
            pair[g, 0] = (product[:n_rows, :n_rows] + product[n_rows:, n_rows:]) * scale
            pair[g, 1] = (product[n_rows:, :n_rows] - product[:n_rows, n_rows:]) * scale
            for b in range(n_stn):
                slabs = slabs_of(pair, g, b)
                for d in range(reach):
                    mine[b, d, step * sub_groups + g] = flatten(slabs, (b + d) % n_stn)
        back_own_copy(step).start()

        def send(n, d):
            @pl.when(owed(stn, lax.rem(stn + n, n_stn), d))
            def _():
                going_back(n, d, step).start()

        each_back(send)
        return carry

    for chunk in range(chunks):
        near_own_copy(chunk).wait()
        for n in range(len(near_turns)):
            near_outgoing(n, chunk).wait_recv()

    near_rows = half * n_chan * SUB

    def near_step(step, carry):
        rows = stack(near, step)
        for g in range(sub_groups):
            product = products(rows, g)
            turned = pltpu.roll(product, near_rows, 1)
            near_pair[g, 0] = (product[:near_rows] + turned[near_rows:]) * scale
            near_pair[g, 1] = (product[near_rows:] - turned[:near_rows]) * scale
            for b in range(half):
                slabs = slabs_of(near_pair, g, b)
                for d in range(half - b):
                    near_mine[b, d, step * sub_groups + g] = flatten(slabs, b + d)
        for d in range(half):

            @pl.when(stays(stn, d))
            def _():
                near_back_own_copy(d, step).start()

            for a in range(1, half):

                @pl.when(stays(neighbour(a), d))
                def _():
                    near_going_back(a, d, step).start()

        return carry

    lax.fori_loop(0, steps, near_step, 0)

    for chunk in range(chunks):
        own_copy(chunk).wait()
        for n in range(len(turns)):
            outgoing(n, chunk).wait_recv()

    lax.fori_loop(0, steps, one_step, 0)

    for chunk in range(chunks):
        for n in range(len(turns)):
            outgoing(n, chunk).wait_send()
        for n in range(len(near_turns)):
            near_outgoing(n, chunk).wait_send()

    def finish(step, carry):
        back_own_copy(step).wait()

        def end(n, d):
            @pl.when(owed(stn, lax.rem(stn + n, n_stn), d))
            def _():
                going_back(n, d, step).wait_send()

            @pl.when(owed(lax.rem(stn - n + n_stn, n_stn), stn, d))
            def _():
                going_back(n, d, step).wait_recv()

        each_back(end)
        for d in range(half):

            @pl.when(stays(stn, d))
            def _():
                near_back_own_copy(d, step).wait()

            for a in range(1, half):

                @pl.when(stays(neighbour(a), d))
                def _():
                    near_going_back(a, d, step).wait_send()

                @pl.when(stays(stn, d))
                def _():
                    near_going_back(a, d, step).wait_recv()

        return carry

    lax.fori_loop(0, steps, finish, 0)


def fused(voltages, taps, n_stn, n_chan):
    inputs_here, frame_count, frame_len = voltages.shape
    count = frame_count - taps.shape[0] + 1
    outer = frame_len // LANES
    kept = frame_len // 2 // outer
    per_chunk = 2 * LANES // outer
    chunks = count // per_chunk
    width = per_chunk * outer
    peers = n_stn * n_chan - 1
    steps = kept // (n_stn * n_chan)
    sub_groups = outer // AVG
    half = n_stn // 2
    reach = half + 1
    groups = kept // n_chan * sub_groups
    mask = (np.arange(count * outer) % outer // AVG)[None, :] == np.arange(sub_groups)[:, None]
    mask = np.broadcast_to(mask[:, None, :], (sub_groups, TILE, count * outer)).astype(jnp.bfloat16)
    tables = [jnp.asarray(t) for t in (*fourier_tables(frame_len), mask)]
    frames_first = jnp.transpose(voltages, (1, 0, 2))
    vmem = pl.BlockSpec(memory_space=pltpu.VMEM)
    return pl.pallas_call(
        functools.partial(fused_kernel, n_stn, n_chan),
        in_specs=[pl.BlockSpec(memory_space=pltpu.HBM)] * (2 + len(tables)),
        out_specs=vmem,
        out_shape=jax.ShapeDtypeStruct((reach, groups, TILE, LANES), jnp.bfloat16),
        scratch_shapes=[pltpu.VMEM(a.shape, a.dtype) for a in (frames_first, taps, *tables)]
        + [
            pltpu.SemaphoreType.DMA((7,)),
            pltpu.VMEM((per_chunk * inputs_here * outer, LANES), jnp.float32),
            pltpu.VMEM((width // LANES, kept * TILE, LANES), jnp.float32),
            pltpu.VMEM((chunks, kept, TILE, width), jnp.bfloat16),
            pltpu.VMEM((chunks, n_stn * n_chan, steps, TILE, width), jnp.bfloat16),
            pltpu.VMEM((sub_groups, 2, LANES, LANES), jnp.float32),
            pltpu.VMEM((n_stn, reach, steps * sub_groups, TILE, LANES), jnp.bfloat16),
            pltpu.SemaphoreType.DMA((chunks,)),
            pltpu.SemaphoreType.DMA((peers, chunks)),
            pltpu.SemaphoreType.DMA((peers, chunks)),
            pltpu.SemaphoreType.DMA((steps,)),
            pltpu.SemaphoreType.DMA((n_stn - 1, reach, steps)),
            pltpu.SemaphoreType.DMA((n_stn - 1, reach, steps)),
            pltpu.VMEM((chunks, half * n_chan, steps, TILE, width), jnp.bfloat16),
            pltpu.VMEM((sub_groups, 2, half * n_chan * SUB, LANES), jnp.float32),
            pltpu.VMEM((half, half, steps * sub_groups, TILE, LANES), jnp.bfloat16),
            pltpu.SemaphoreType.DMA((chunks,)),
            pltpu.SemaphoreType.DMA((half * n_chan - 1, chunks)),
            pltpu.SemaphoreType.DMA((half * n_chan - 1, chunks)),
            pltpu.SemaphoreType.DMA((half, steps)),
            pltpu.SemaphoreType.DMA((half - 1, half, steps)),
            pltpu.SemaphoreType.DMA((half - 1, half, steps)),
        ],
        compiler_params=pltpu.CompilerParams(
            collective_id=0, has_side_effects=True, vmem_limit_bytes=63 * 2**20
        ),
    )(frames_first, taps, *tables)


def local(voltages, taps):
    inputs_here, frame_count, frame_len = voltages.shape
    count = frame_count - taps.shape[0] + 1
    n_stn, n_chan = lax.axis_size("stn"), lax.axis_size("chan")
    outer = frame_len // LANES
    fits = (
        inputs_here == SUB
        and inputs_here * n_stn * n_chan == LANES
        and frame_len % (LANES * AVG) == 0
        and LANES % outer == 0
        and count % (2 * LANES // outer) == 0
        and count % TILE == 0
        and n_stn % 2 == 0
        and n_stn > 2
        and count > 2 * LANES // outer
        and frame_len // 2 // outer % (n_stn * n_chan) == 0
        and (inputs_here * n_chan) ** 2 == SUB * LANES
    )
    if not fits:
        return general(voltages, taps)
    tiles = fused(voltages, taps, n_stn, n_chan)
    reach, groups = tiles.shape[:2]
    return tiles.reshape(1, reach, groups, 2, (inputs_here * n_chan) ** 2)


def solution(mesh):
    placed = (P(("grp", "stn", "chan"), None, None), P())
    return jax.shard_map(
        local,
        mesh=mesh,
        in_specs=placed,
        out_specs=P(("grp", "stn"), None, "chan", None, None),
        check_vma=False,
    )
```
